512 devices in a mesh: wall: 16 (over x, y_hi, core), space: 32 (over y_lo, z).
Axes of the slice: x: 4, y: 8 (y_hi: 2, y_lo: 4; y = y_hi * 4 + y_lo), z: 8, core: 2. Of those that a mesh axis runs over, the one named last changes fastest.
Arguments:
- velocity: float32 [16, 2048, 1024], P('wall', 'space'), may hold values from -6 to 6
Outputs:
- correlation: float32 [16, 1, 2048, 1024], P('wall', None, 'space')
The draws below stay inside these ranges and needn't reach their ends.
All inputs are finite; a program needn't handle non-finite values.
Results may differ from the reference program's by a relative error of at most 0.0003.
Values sent between devices are 32-bit elements; how exact they have to be, the bound alone decides.
A program may use at most 64 MiB of HBM per device.

```python
import jax
import jax.numpy as jnp
from jax import lax

NX = 2048
NZ = 1024
PL = 1
NY = 16
N_WALL = 16


def level_of(stream_key, shape, cuts, smallest, largest):
    def one(position, shards_of):
        heights = jax.random.uniform(jax.random.fold_in(jax.random.fold_in(stream_key, 6), position), (shards_of,), jnp.float32, smallest / len(cuts), largest / len(cuts))
        return jnp.repeat(jnp.exp(heights), shape[position] // shards_of).reshape((-1,) + (1,) * (len(shape) - position - 1))

    factor_of = one(*cuts[0])
    for cut in cuts[1:]:
        factor_of = factor_of * one(*cut)
    return factor_of


def bell_draw(key, shape, scale, reach, split=(), kind=jnp.bfloat16):
    factor_of = level_of(key, shape, split, -0.22, 0.18) if split else 1.0
    drawn = jax.random.normal(key, shape, jnp.float32) * scale * factor_of
    return jnp.minimum(jnp.maximum(drawn, -reach), reach).astype(kind)


def setup_inputs(seed: int = 0) -> dict:
    key_of = jax.random.split(jax.random.key(seed), 2)
    velocity = bell_draw(key_of[0], (NY, NX, NZ), 1.0, 6.0, ((0, 16), (1, 32)), jnp.float32)
    return {"velocity": velocity}


def reference(velocity):
    spectra = jnp.fft.fft2(velocity, axes=(1, 2))
    scale_factor = (NX * NZ) ** -0.5

    def one_plane(plane_index):
        own_block = plane_index // PL
        partner_block = (own_block + N_WALL // 2) % N_WALL
        others = lax.dynamic_slice_in_dim(spectra, (partner_block * PL).astype(jnp.int32), PL, 0)
        own_spectrum = lax.dynamic_slice_in_dim(spectra, plane_index.astype(jnp.int32), 1, 0)
        cross_term = jnp.conj(own_spectrum) * others
        return jnp.real(jnp.fft.ifft2(cross_term, axes=(1, 2))) * scale_factor

    result = lax.map(one_plane, jnp.arange(NY, dtype=jnp.int32))
    return result.astype(jnp.float32)
```

```python
import math

import jax
import jax.numpy as jnp
import ml_dtypes
import numpy as np
from jax import lax
from jax.experimental import pallas as pl
from jax.experimental.pallas import tpu as pltpu
from jax.sharding import PartitionSpec as P

F32 = jnp.float32
BF16 = jnp.bfloat16
HALF = math.sqrt(0.5)

NX, NZ = 2048, 1024
SPREAD, ROWS = 32, 64
PEERS = 2 * SPREAD
TILE = 8


def split_table(table):
    high = table.astype(ml_dtypes.bfloat16)
    low = (table - high.astype(np.float64)).astype(ml_dtypes.bfloat16)
    return high, low


def mode_of(block, n):
    if block:
        return 8 * n + block
    return np.where(n < 64, 8 * n, 8 * (n - 64) + 4)


def slots():
    kb, dev, part, ka = np.meshgrid(np.arange(2), np.arange(16), np.arange(2), np.arange(4), indexing="ij")
    return dev * 8 + ka * 2 + kb, part


def span_forward_tables():
    n, part = slots()
    n, part = n[..., None], part[..., None]
    zi = np.arange(128)
    out = np.zeros((4, 2, 128, 256))
    for block in range(4):
        angle = 2 * np.pi * (mode_of(block, n) * zi % NZ) / NZ
        cos, sin = np.cos(angle), np.sin(angle)
        from_re = np.where(part == 0, cos, -sin)
        from_im = np.where(part == 0, sin, cos)
        if block == 0:
            alternate = np.where(zi % 2 == 0, 1.0, -1.0)
            from_re = np.where((n == 0) & (part == 1), alternate, from_re)
            first = np.where(n < 64, from_re, 0.0)
            second = np.where(n < 64, 0.0, from_re)
        else:
            first, second = from_re, from_im
        out[block] = np.concatenate([first, second], axis=-1).reshape(2, 128, 256)
    high, low = split_table(out)
    return np.concatenate([high, low], axis=2)


def span_inverse_tables():
    n, part = slots()
    n, part = n[..., None], part[..., None]
    zi = np.arange(128)
    scale = (NX * NZ) ** -1.5
    out = np.zeros((4, 256, 256))
    for block in range(4):
        angle = 2 * np.pi * (mode_of(block, n) * zi % NZ) / NZ
        cos, sin = np.cos(angle), np.sin(angle)
        to_re = 2 * np.where(part == 0, cos, -sin)
        to_im = 2 * np.where(part == 0, sin, cos)
        if block == 0:
            alternate = np.where(zi % 2 == 0, 1.0, -1.0)
            to_re = np.where(n == 0, np.where(part == 0, 1.0, alternate), to_re)
            first = np.where(n < 64, to_re, 0.0)
            second = np.where(n < 64, 0.0, to_re)
        else:
            first, second = to_re, to_im
        out[block] = np.concatenate([first, second], axis=-1).reshape(256, 256) * scale
    high, low = split_table(out)
    return np.stack([high, low], axis=1)


def stream_outer_forward():
    out = np.zeros((2, 160, SPREAD, 2, 4))
    t, s = np.arange(SPREAD)[:, None], np.arange(SPREAD)[None, :]
    cos, sin = np.cos(2 * np.pi * (t * s % 32) / 32), np.sin(2 * np.pi * (t * s % 32) / 32)
    for ka in range(4):
        rows = slice(32 * ka, 32 * ka + 32)
        out[0, rows, :, 0, ka] = cos
        out[0, rows, :, 1, ka] = sin
        out[1, rows, :, 0, ka] = -sin
        out[1, rows, :, 1, ka] = cos
    out[0, 128:, :, 0, 0] = cos
    out[0, 128:, :, 1, 0] = -sin
    out[1, 128:, :, 0, 0] = -sin
    out[1, 128:, :, 1, 0] = -cos
    return np.stack(split_table(out.reshape(320, 256)))


def stream_outer_inverse():
    out = np.zeros((SPREAD, 2, 4, 2, 4, SPREAD))
    s, t = np.arange(SPREAD)[:, None], np.arange(SPREAD)[None, :]
    cos, sin = np.cos(2 * np.pi * (t * s % 32) / 32), np.sin(2 * np.pi * (t * s % 32) / 32)
    for ka in range(4):
        out[:, 0, ka, 0, ka] = cos
        out[:, 0, ka, 1, ka] = -sin
        out[:, 1, ka, 0, ka] = sin
        out[:, 1, ka, 1, ka] = cos
    return np.stack(split_table(out.reshape(256, 256)))


def stream_inner(sign):
    out = np.zeros((2, 2, ROWS, 2, 2, ROWS))
    r, m = np.arange(ROWS)[:, None], np.arange(ROWS)[None, :]
    cos, sin = np.cos(2 * np.pi * (r * m % 64) / 64), sign * np.sin(2 * np.pi * (r * m % 64) / 64)
    for kb in range(2):
        out[0, kb, :, 0, kb] = cos
        out[1, kb, :, 0, kb] = -sin
        out[0, kb, :, 1, kb] = sin
        out[1, kb, :, 1, kb] = cos
    return np.stack(split_table(out.reshape(256, 256)))


def twist_tables():
    t = np.tile(np.arange(SPREAD), 5)[:, None]
    r = np.tile(np.arange(ROWS), 2)[None, :]
    angle = 2 * np.pi * (t * r) / NX
    return np.stack([np.cos(angle), np.sin(angle)]).astype(np.float32)


def split(x):
    high = x.astype(BF16)
    return high, (x - high.astype(F32)).astype(BF16)


def mul(a, b):
    return jnp.dot(a, b, preferred_element_type=F32)


def mul_nt(a, b):
    return lax.dot_general(a, b, (((1,), (1,)), ((), ())), preferred_element_type=F32)


def kernel(
    u_hbm, wf_hbm, k1_hbm, d1_hbm, tw_hbm, d2_hbm, k2_hbm, wi_hbm, out_ref,
    u, wf, k1, d1, tw, d2, k2, wi, e_high, e_low, send1, recv1, send2, recv2,
    load_sem, send_sem, recv_sem,
):
    wall, space = lax.axis_index("wall"), lax.axis_index("space")
    pairs = lax.axis_size("wall") // 2
    plane = wall // pairs
    base = lax.rem(wall, pairs)
    y, z = space // 8, lax.rem(space, 8)
    me_mode = y * 16 + plane * 8 + z
    me_row = plane * SPREAD + space

    loads = []
    for i, (src, dst) in enumerate(
        [(u_hbm, u), (wf_hbm, wf), (k1_hbm, k1), (d1_hbm, d1), (tw_hbm, tw), (d2_hbm, d2), (k2_hbm, k2), (wi_hbm, wi)]
    ):
        loads.append(pltpu.make_async_copy(src, dst, load_sem.at[i]))
        loads[-1].start()

    barrier = pltpu.get_barrier_semaphore()

    def greet(i, carry):
        other = lax.rem(me_row + i, PEERS)
        pl.semaphore_signal(
            barrier, inc=1, device_id={"wall": base + pairs * (other // SPREAD), "space": lax.rem(other, SPREAD)},
            device_id_type=pl.DeviceIdType.MESH,
        )
        return carry

    lax.fori_loop(1, PEERS, greet, 0)

    def tile(ref, index):
        return ref.at[pl.ds(pl.multiple_of(index * TILE, TILE), TILE)]

    def send(stage, src, dst, to_plane, to_space):
        return pltpu.make_async_remote_copy(
            src_ref=src, dst_ref=dst, send_sem=send_sem.at[stage], recv_sem=recv_sem.at[stage],
            device_id={"wall": base + pairs * to_plane, "space": to_space},
            device_id_type=pl.DeviceIdType.MESH,
        )

    loads[0].wait()
    parts = [u[0, :, 128 * b : 128 * b + 128] for b in range(8)]
    plus = [parts[b] + parts[b + 4] for b in range(4)]
    minus = [parts[b] - parts[b + 4] for b in range(4)]
    even, odd = plus[0] + plus[2], plus[1] + plus[3]
    across, along = (minus[1] - minus[3]) * HALF, (minus[1] + minus[3]) * HALF
    eighths = [
        (even + odd, even - odd),
        (minus[0] + across, -minus[2] - along),
        (plus[0] - plus[2], plus[3] - plus[1]),
        (minus[0] - across, minus[2] - along),
    ]
    for block, (first, second) in enumerate(eighths):
        for half, value in enumerate((first, second)):
            high, low = split(value)
            e_high[block, :, 128 * half : 128 * half + 128] = high
            e_low[block, :, 128 * half : 128 * half + 128] = low

    loads[1].wait()
    nothing = jnp.zeros((ROWS, 256), BF16)
    for step in range(4):
        block = lax.rem(y + 2 + step, 4)
        high, low = e_high[block], e_low[block]
        both = mul_nt(wf[block, 0], jnp.concatenate([high, nothing, low, nothing], axis=0))
        both += mul_nt(wf[block, 1], jnp.concatenate([nothing, high, nothing, low], axis=0))
        send1[pl.ds(pl.multiple_of(block * 128, 128), 128), :] = both[:128, :128] + both[:128, 128:] + both[128:, :128]
        if step == 0:
            pl.semaphore_wait(barrier, PEERS - 1)

        def send_block(j, carry):
            to_plane = lax.rem(plane + 1 + j // 8, 2)
            to_z = lax.rem(z + 4 + j, 8)
            to = block * 16 + to_plane * 8 + to_z

            @pl.when(to != me_mode)
            def _():
                send(0, tile(send1, to), tile(recv1, me_row), to_plane, block * 8 + to_z).start()

            return carry

        lax.fori_loop(0, 16, send_block, 0)
    own1 = pltpu.make_async_copy(tile(send1, me_mode), tile(recv1, me_row), recv_sem.at[0])
    own1.start()
    for load in loads[2:]:
        load.wait()
    pltpu.make_async_copy(recv1, recv1, recv_sem.at[0]).wait()

    high, low = split(recv1[...])
    h = [high[:256], high[256:]]
    l = [low[:256], low[256:]]
    outer = mul(k1[0], jnp.concatenate([h[0], l[0], h[1], l[1]], axis=1))
    outer_low = mul(k1[1], jnp.concatenate(h, axis=1))
    cos, sin = tw[0], tw[1]
    turned = []
    for p in range(2):
        got = outer[:, 256 * p : 256 * p + 128] + outer[:, 256 * p + 128 : 256 * p + 256] + outer_low[:, 128 * p : 128 * p + 128]
        re, im = got[:160], got[160:]
        turned.append(jnp.concatenate([re * cos + im * sin, im * cos - re * sin], axis=1))
    high, low = split(jnp.concatenate(turned, axis=0))
    both = mul(jnp.concatenate([high, low], axis=0), d1[0])
    spectra = both[:320] + both[320:] + mul(high, d1[1])

    a_re, a_im = spectra[:128, :128], spectra[:128, 128:]
    b_re, b_im = spectra[160:288, :128], spectra[160:288, 128:]
    cross_re = a_re * b_re + a_im * b_im
    cross_im = a_re * b_im - a_im * b_re

    def unpack(column, mirror):
        c_re, c_im = column[:, :128], column[:, 128:]
        m_re, m_im = mirror[:, :128], mirror[:, 128:]
        return (c_re + m_re) * 0.5, (c_im + m_im) * 0.5, (c_im - m_im) * 0.5, (m_re - c_re) * 0.5

    a0_re, a0_im, a1_re, a1_im = unpack(spectra[:32], spectra[128:160])
    b0_re, b0_im, b1_re, b1_im = unpack(spectra[160:192], spectra[288:320])
    zero_re, zero_im = a0_re * b0_re + a0_im * b0_im, a0_re * b0_im - a0_im * b0_re
    last_re, last_im = a1_re * b1_re + a1_im * b1_im, a1_re * b1_im - a1_im * b1_re
    lane = lax.broadcasted_iota(jnp.int32, (32, 128), 1)
    packed = jnp.logical_and(lane < ROWS, me_mode == 0)

    def merge(special, plain):
        return jnp.concatenate([jnp.where(packed, special, plain[:32]), plain[32:]], axis=0)

    first = jnp.concatenate([merge(zero_re - last_im, cross_re), merge(zero_im + last_re, cross_im)], axis=1)
    second = jnp.concatenate([merge(zero_re + last_im, cross_re), merge(last_re - zero_im, -cross_im)], axis=1)

    high, low = split(jnp.concatenate([first, second], axis=0))
    both = mul(jnp.concatenate([high, low], axis=0), d2[0])
    inner = both[:256] + both[256:] + mul(high, d2[1])
    cos, sin = cos[:128], sin[:128]
    columns, columns_high = [], []
    for p in range(2):
        re, im = inner[128 * p : 128 * p + 128, :128], inner[128 * p : 128 * p + 128, 128:]
        high, low = split(jnp.concatenate([re * cos - im * sin, im * cos + re * sin], axis=0))
        columns += [high, low]
        columns_high.append(high)
    outer = mul(k2[0], jnp.concatenate(columns, axis=1))
    outer_low = mul(k2[1], jnp.concatenate(columns_high, axis=1))
    for p in range(2):
        send2[256 * p : 256 * p + 256, :] = (
            outer[:, 256 * p : 256 * p + 128] + outer[:, 256 * p + 128 : 256 * p + 256] + outer_low[:, 128 * p : 128 * p + 128]
        )

    def send_back(j, carry):
        to_plane = lax.rem(plane + 1 + j // SPREAD, 2)
        to_y = lax.rem(y + 2 + lax.rem(j, SPREAD) // 8, 4)
        to_z = lax.rem(z + 4 + j, 8)
        to_space = to_y * 8 + to_z
        to = to_plane * SPREAD + to_space

        @pl.when(to != me_row)
        def _():
            send(1, tile(send2, to), tile(recv2, me_mode), to_plane, to_space).start()

        return carry

    lax.fori_loop(0, PEERS, send_back, 0)
    own2 = pltpu.make_async_copy(tile(send2, me_row), tile(recv2, me_mode), recv_sem.at[1])
    own2.start()
    pltpu.make_async_copy(recv2, recv2, recv_sem.at[1]).wait()

    fields = []
    for block in range(4):
        flat = recv2[128 * block : 128 * block + 128, :].T
        high, low = split(jnp.concatenate([flat[:ROWS], flat[ROWS:]], axis=1))
        both = mul(jnp.concatenate([high, low], axis=0), wi[block, 0])
        fields.append(both[:ROWS] + both[ROWS:] + mul(high, wi[block, 1]))
    (h0, h4), (r1, i1), (r2, i2), (r3, i3) = [(f[:, :128], f[:, 128:]) for f in fields]
    sums, differences = h0 + h4, h0 - h4
    evens = [sums + r2, differences - i2, sums - r2, differences + i2]
    odds = [r1 + r3, (r1 - r3 - i1 - i3) * HALF, i3 - i1, (r3 - r1 - i1 - i3) * HALF]
    for b in range(4):
        out_ref[0, 0, :, 128 * b : 128 * b + 128] = evens[b] + odds[b]
        out_ref[0, 0, :, 128 * b + 512 : 128 * b + 640] = evens[b] - odds[b]

    count = (PEERS - 1) * TILE
    for stage, buffer in enumerate((send1, send2)):
        pltpu.make_async_copy(buffer.at[pl.ds(0, count)], buffer.at[pl.ds(0, count)], send_sem.at[stage]).wait()


def local(velocity):
    tables = [
        span_forward_tables(), stream_outer_forward(), stream_inner(-1.0), twist_tables(),
        stream_inner(1.0), stream_outer_inverse(), span_inverse_tables(),
    ]
    tables = [jnp.asarray(t) for t in tables]
    messages = pltpu.VMEM((PEERS * TILE, 128), F32)
    return pl.pallas_call(
        kernel,
        out_shape=jax.ShapeDtypeStruct((1, 1, ROWS, NZ), F32),
        in_specs=[pl.BlockSpec(memory_space=pl.ANY)] * 8,
        out_specs=pl.BlockSpec(memory_space=pltpu.VMEM),
        scratch_shapes=[pltpu.VMEM(velocity.shape, F32)]
        + [pltpu.VMEM(t.shape, t.dtype) for t in tables]
        + [pltpu.VMEM((4, ROWS, 256), BF16)] * 2
        + [messages] * 4
        + [pltpu.SemaphoreType.DMA((8,)), pltpu.SemaphoreType.DMA((2,)), pltpu.SemaphoreType.DMA((2,))],
        compiler_params=pltpu.CompilerParams(
            collective_id=0, has_side_effects=True, vmem_limit_bytes=32 * 1024 * 1024
        ),
    )(velocity, *tables)


def solution(mesh):
    return jax.shard_map(
        local, mesh=mesh, in_specs=(P("wall", "space", None),), out_specs=P("wall", None, "space", None), check_vma=False
    )
```

```python
import math

import jax
import jax.numpy as jnp
import ml_dtypes
import numpy as np
from jax import lax
from jax.experimental import pallas as pl
from jax.experimental.pallas import tpu as pltpu
from jax.sharding import PartitionSpec as P

F32 = jnp.float32
BF16 = jnp.bfloat16
HALF = math.sqrt(0.5)

NX, NZ = 2048, 1024
SPREAD, ROWS = 32, 64
PEERS = 2 * SPREAD
TILE = 8


def split_table(table):
    high = table.astype(ml_dtypes.bfloat16)
    low = (table - high.astype(np.float64)).astype(ml_dtypes.bfloat16)
    return high, low


def mode_of(block, n):
    if block:
        return 8 * n + block
    return np.where(n < 64, 8 * n, 8 * (n - 64) + 4)


def slots():
    kb, dev, chunk, part, ka = np.meshgrid(*map(np.arange, (2, 16, 2, 2, 2)), indexing="ij")
    return dev * 8 + chunk * 4 + ka * 2 + kb, part


def span_forward_tables():
    n, part = slots()
    n, part = n[..., None], part[..., None]
    zi = np.arange(128)
    out = np.zeros((4, 2, 128, 256))
    for block in range(4):
        angle = 2 * np.pi * (mode_of(block, n) * zi % NZ) / NZ
        cos, sin = np.cos(angle), np.sin(angle)
        from_re = np.where(part == 0, cos, -sin)
        from_im = np.where(part == 0, sin, cos)
        if block == 0:
            alternate = np.where(zi % 2 == 0, 1.0, -1.0)
            from_re = np.where((n == 0) & (part == 1), alternate, from_re)
            first = np.where(n < 64, from_re, 0.0)
            second = np.where(n < 64, 0.0, from_re)
        else:
            first, second = from_re, from_im
        out[block] = np.concatenate([first, second], axis=-1).reshape(2, 128, 256)
    high, low = split_table(out)
    return np.concatenate([high, low], axis=2)


def span_inverse_tables():
    n, part = slots()
    n, part = n[..., None], part[..., None]
    zi = np.arange(128)
    scale = (NX * NZ) ** -1.5
    out = np.zeros((4, 256, 256))
    for block in range(4):
        angle = 2 * np.pi * (mode_of(block, n) * zi % NZ) / NZ
        cos, sin = np.cos(angle), np.sin(angle)
        to_re = 2 * np.where(part == 0, cos, -sin)
        to_im = 2 * np.where(part == 0, sin, cos)
        if block == 0:
            alternate = np.where(zi % 2 == 0, 1.0, -1.0)
            to_re = np.where(n == 0, np.where(part == 0, 1.0, alternate), to_re)
            first = np.where(n < 64, to_re, 0.0)
            second = np.where(n < 64, 0.0, to_re)
        else:
            first, second = to_re, to_im
        out[block] = np.concatenate([first, second], axis=-1).reshape(256, 256) * scale
    high, low = split_table(out)
    return np.stack([high, low], axis=1)


def stream_outer_forward():
    out = np.zeros((2, 96, SPREAD, 8))
    t, s = np.arange(SPREAD)[:, None], np.arange(SPREAD)[None, :]
    cos, sin = np.cos(2 * np.pi * (t * s % 32) / 32), np.sin(2 * np.pi * (t * s % 32) / 32)
    for ka in range(2):
        rows = slice(32 * ka, 32 * ka + 32)
        out[0, rows, :, ka] = cos
        out[0, rows, :, 2 + ka] = sin
        out[1, rows, :, ka] = -sin
        out[1, rows, :, 2 + ka] = cos
    out[0, 64:, :, 0] = cos
    out[0, 64:, :, 2] = -sin
    out[1, 64:, :, 0] = -sin
    out[1, 64:, :, 2] = -cos
    return np.stack(split_table(out.reshape(192, 256)))


def stream_outer_inverse():
    out = np.zeros((SPREAD, 2, 2, 2, 2, SPREAD))
    s, t = np.arange(SPREAD)[:, None], np.arange(SPREAD)[None, :]
    cos, sin = np.cos(2 * np.pi * (t * s % 32) / 32), np.sin(2 * np.pi * (t * s % 32) / 32)
    for ka in range(2):
        out[:, 0, ka, 0, ka] = cos
        out[:, 0, ka, 1, ka] = -sin
        out[:, 1, ka, 0, ka] = sin
        out[:, 1, ka, 1, ka] = cos
    return np.stack(split_table(out.reshape(128, 128)))


def stream_inner(sign):
    out = np.zeros((2, 2, ROWS, 2, 2, ROWS))
    r, m = np.arange(ROWS)[:, None], np.arange(ROWS)[None, :]
    cos, sin = np.cos(2 * np.pi * (r * m % 64) / 64), sign * np.sin(2 * np.pi * (r * m % 64) / 64)
    for kb in range(2):
        out[0, kb, :, 0, kb] = cos
        out[1, kb, :, 0, kb] = -sin
        out[0, kb, :, 1, kb] = sin
        out[1, kb, :, 1, kb] = cos
    return np.stack(split_table(out.reshape(256, 256)))


def twist_tables():
    t = np.tile(np.arange(SPREAD), 3)[:, None]
    r = np.tile(np.arange(ROWS), 2)[None, :]
    angle = 2 * np.pi * (t * r) / NX
    return np.stack([np.cos(angle), np.sin(angle)]).astype(np.float32)


def split(x):
    high = x.astype(BF16)
    return high, (x - high.astype(F32)).astype(BF16)


def mul(a, b):
    return jnp.dot(a, b, preferred_element_type=F32)


def mul_nt(a, b):
    return lax.dot_general(a, b, (((1,), (1,)), ((), ())), preferred_element_type=F32)


def stream_chunk(chunk, recv1, send2, k1, d1, d2, k2, cos, sin, used, me_mode):
    halves = [split(jnp.where(used, recv1[chunk, 256 * p : 256 * p + 256, :], 0.0)) for p in range(2)]
    extra = 32 if chunk == 0 else 0
    rows = 64 + extra

    def table(part):
        return k1[part] if chunk == 0 else jnp.concatenate([k1[part, :64], k1[part, 96:160]], axis=0)

    outer = mul(table(0), jnp.concatenate([x for pair in halves for x in pair], axis=1))
    outer_low = mul(table(1), jnp.concatenate([high for high, _ in halves], axis=1))
    turned = []
    for p in range(2):
        got = outer[:, 256 * p : 256 * p + 128] + outer[:, 256 * p + 128 : 256 * p + 256] + outer_low[:, 128 * p : 128 * p + 128]
        re, im = got[:rows], got[rows:]
        turned.append(jnp.concatenate([re * cos[:rows] + im * sin[:rows], im * cos[:rows] - re * sin[:rows]], axis=1))
    high, low = split(jnp.concatenate(turned, axis=0))
    both = mul(jnp.concatenate([high, low], axis=0), d1[0])
    spectra = both[: 2 * rows] + both[2 * rows :] + mul(high, d1[1])

    a_re, a_im = spectra[:64, :128], spectra[:64, 128:]
    b_re, b_im = spectra[rows : rows + 64, :128], spectra[rows : rows + 64, 128:]
    cross_re = a_re * b_re + a_im * b_im
    cross_im = a_re * b_im - a_im * b_re
    first, second = (cross_re, cross_im), (cross_re, -cross_im)

    if chunk == 0:
        def unpack(column, mirror):
            c_re, c_im = column[:, :128], column[:, 128:]
            m_re, m_im = mirror[:, :128], mirror[:, 128:]
            return (c_re + m_re) * 0.5, (c_im + m_im) * 0.5, (c_im - m_im) * 0.5, (m_re - c_re) * 0.5

        a0_re, a0_im, a1_re, a1_im = unpack(spectra[:32], spectra[64:96])
        b0_re, b0_im, b1_re, b1_im = unpack(spectra[96:128], spectra[160:192])
        zero_re, zero_im = a0_re * b0_re + a0_im * b0_im, a0_re * b0_im - a0_im * b0_re
        last_re, last_im = a1_re * b1_re + a1_im * b1_im, a1_re * b1_im - a1_im * b1_re
        lane = lax.broadcasted_iota(jnp.int32, (32, 128), 1)
        packed = jnp.logical_and(lane < ROWS, me_mode == 0)

        def merge(special, plain):
            return jnp.concatenate([jnp.where(packed, special, plain[:32]), plain[32:]], axis=0)

        first = merge(zero_re - last_im, cross_re), merge(zero_im + last_re, cross_im)
        second = merge(zero_re + last_im, cross_re), merge(last_re - zero_im, -cross_im)

    high, low = split(jnp.concatenate([jnp.concatenate(first, axis=1), jnp.concatenate(second, axis=1)], axis=0))
    both = mul(jnp.concatenate([high, low], axis=0), d2[0])
    inner = both[:128] + both[128:] + mul(high, d2[1])
    cos, sin = cos[:64], sin[:64]
    columns = []
    for p in range(2):
        re, im = inner[64 * p : 64 * p + 64, :128], inner[64 * p : 64 * p + 64, 128:]
        columns.append(split(jnp.concatenate([re * cos - im * sin, im * cos + re * sin], axis=0)))
    outer = mul(k2[0], jnp.concatenate([x for pair in columns for x in pair], axis=1))
    outer_low = mul(k2[1], jnp.concatenate([high for high, _ in columns], axis=1))
    for p in range(2):
        got = outer[:, 256 * p : 256 * p + 128] + outer[:, 256 * p + 128 : 256 * p + 256] + outer_low[:, 128 * p : 128 * p + 128]
        got = got.reshape(16, TILE, 128)
        spaced = jnp.stack([got, pltpu.roll(got, TILE // 2, 1)], axis=1)
        send2[chunk, 256 * p : 256 * p + 256, :] = spaced.reshape(256, 128)


def kernel(
    u_hbm, wf_hbm, k1_hbm, d1_hbm, tw_hbm, d2_hbm, k2_hbm, wi_hbm, out_ref,
    u, wf, k1, d1, tw, d2, k2, wi, e_high, e_low, send1, recv1, send2, recv2,
    load_sem, send_sem, recv_sem,
):
    wall, space = lax.axis_index("wall"), lax.axis_index("space")
    pairs = lax.axis_size("wall") // 2
    plane = wall // pairs
    base = lax.rem(wall, pairs)
    y, z = space // 8, lax.rem(space, 8)
    me_mode = y * 16 + plane * 8 + z
    me_row = plane * SPREAD + space

    loads = []
    for i, (src, dst) in enumerate(
        [(u_hbm, u), (wf_hbm, wf), (k1_hbm, k1), (d1_hbm, d1), (tw_hbm, tw), (d2_hbm, d2), (k2_hbm, k2), (wi_hbm, wi)]
    ):
        loads.append(pltpu.make_async_copy(src, dst, load_sem.at[i]))
        loads[-1].start()

    def address(to_plane, to_space):
        return {"device_id": {"wall": base + pairs * to_plane, "space": to_space}, "device_id_type": pl.DeviceIdType.MESH}

    def others(to_z, skip_self=False):
        for dy in (2, 3, 1, 0):
            for flip in (1, 0):
                if not (skip_self and flip == dy == 0):
                    yield lax.rem(plane + flip, 2), lax.rem(y + dy, 4) * 8 + to_z

    def everyone(act):
        @pl.loop(0, 7)
        def _(i):
            act(lax.rem(z + 4 + (1 - 2 * lax.rem(i, 2)) * ((i + 1) // 2), 8))

        act(z, skip_self=True)

    barrier = pltpu.get_barrier_semaphore()

    def greet(to_z, skip_self=False):
        for peer in others(to_z, skip_self):
            pl.semaphore_signal(barrier, inc=1, **address(*peer))

    everyone(greet)

    def tile(ref, index):
        return ref.at[pl.ds(pl.multiple_of(index * TILE, TILE), TILE // 2)]

    def exchange(stage, src, dst, place_there, place_here):
        def send(to_z, skip_self=False):
            for to_plane, to_space in others(to_z, skip_self):
                pltpu.make_async_remote_copy(
                    src_ref=tile(src, place_there(to_plane, to_space)), dst_ref=tile(dst, place_here),
                    send_sem=send_sem.at[stage], recv_sem=recv_sem.at[stage], **address(to_plane, to_space),
                ).start()

        everyone(send)
        pltpu.make_async_copy(tile(src, place_there(plane, space)), tile(dst, place_here), recv_sem.at[stage]).start()

    def wait_tiles(sem, count):
        rows = send1.at[0].at[pl.ds(0, count * TILE // 2)]
        pltpu.make_async_copy(rows, rows, sem).wait()

    def mode_place(of_plane, of_space):
        return (of_space // 8) * 16 + of_plane * 8 + lax.rem(of_space, 8)

    def row_place(of_plane, of_space):
        return of_plane * SPREAD + of_space

    loads[0].wait()
    parts = [u[0, :, 128 * b : 128 * b + 128] for b in range(8)]
    plus = [parts[b] + parts[b + 4] for b in range(4)]
    minus = [parts[b] - parts[b + 4] for b in range(4)]
    even, odd = plus[0] + plus[2], plus[1] + plus[3]
    across, along = (minus[1] - minus[3]) * HALF, (minus[1] + minus[3]) * HALF
    eighths = [
        (even + odd, even - odd),
        (minus[0] + across, -minus[2] - along),
        (plus[0] - plus[2], plus[3] - plus[1]),
        (minus[0] - across, minus[2] - along),
    ]
    for block, (first, second) in enumerate(eighths):
        for half, value in enumerate((first, second)):
            high, low = split(value)
            e_high[block, :, 128 * half : 128 * half + 128] = high
            e_low[block, :, 128 * half : 128 * half + 128] = low

    loads[1].wait()
    nothing = jnp.zeros((ROWS, 256), BF16)
    for block in range(4):
        high, low = e_high[block], e_low[block]
        both = mul_nt(wf[block, 0], jnp.concatenate([high, nothing, low, nothing], axis=0))
        both += mul_nt(wf[block, 1], jnp.concatenate([nothing, high, nothing, low], axis=0))
        got = both[:128, :128] + both[:128, 128:] + both[128:, :128]
        send1[0, 128 * block : 128 * block + 128, :] = got
        got = pltpu.roll(got.reshape(16, TILE, 128), TILE // 2, 1)
        send1[1, 128 * block : 128 * block + 128, :] = got.reshape(128, 128)

    pl.semaphore_wait(barrier, PEERS - 1)
    for chunk in range(2):
        exchange(chunk, send1.at[chunk], recv1.at[chunk], mode_place, me_row)
    for load in loads[2:]:
        load.wait()

    cos, sin = tw[0], tw[1]
    used = lax.broadcasted_iota(jnp.int32, (256, 128), 0) % TILE < TILE // 2
    for chunk in range(2):
        wait_tiles(recv_sem.at[chunk], PEERS)
        stream_chunk(chunk, recv1, send2, k1, d1, d2, k2, cos, sin, used, me_mode)
        exchange(2 + chunk, send2.at[chunk], recv2.at[chunk], row_place, me_mode)
    for chunk in range(2):
        wait_tiles(recv_sem.at[2 + chunk], PEERS)

    upper = lax.broadcasted_iota(jnp.int32, (16, TILE, 128), 1) < TILE // 2
    fields = []
    for block in range(4):
        first, second = [recv2[c, 128 * block : 128 * block + 128, :].reshape(16, TILE, 128) for c in range(2)]
        flat = jnp.where(upper, first, pltpu.roll(second, TILE // 2, 1)).reshape(128, 128).T
        high, low = split(jnp.concatenate([flat[:ROWS], flat[ROWS:]], axis=1))
        both = mul(jnp.concatenate([high, low], axis=0), wi[block, 0])
        fields.append(both[:ROWS] + both[ROWS:] + mul(high, wi[block, 1]))
    (h0, h4), (r1, i1), (r2, i2), (r3, i3) = [(f[:, :128], f[:, 128:]) for f in fields]
    sums, differences = h0 + h4, h0 - h4
    evens = [sums + r2, differences - i2, sums - r2, differences + i2]
    odds = [r1 + r3, (r1 - r3 - i1 - i3) * HALF, i3 - i1, (r3 - r1 - i1 - i3) * HALF]
    for b in range(4):
        out_ref[0, 0, :, 128 * b : 128 * b + 128] = evens[b] + odds[b]
        out_ref[0, 0, :, 128 * b + 512 : 128 * b + 640] = evens[b] - odds[b]

    for stage in range(4):
        wait_tiles(send_sem.at[stage], PEERS - 1)


def local(velocity):
    tables = [
        span_forward_tables(), stream_outer_forward(), stream_inner(-1.0), twist_tables(),
        stream_inner(1.0), stream_outer_inverse(), span_inverse_tables(),
    ]
    tables = [jnp.asarray(t) for t in tables]
    messages = pltpu.VMEM((2, PEERS * TILE, 128), F32)
    return pl.pallas_call(
        kernel,
        out_shape=jax.ShapeDtypeStruct((1, 1, ROWS, NZ), F32),
        in_specs=[pl.BlockSpec(memory_space=pl.ANY)] * 8,
        out_specs=pl.BlockSpec(memory_space=pltpu.VMEM),
        scratch_shapes=[pltpu.VMEM(velocity.shape, F32)]
        + [pltpu.VMEM(t.shape, t.dtype) for t in tables]
        + [pltpu.VMEM((4, ROWS, 256), BF16)] * 2
        + [messages] * 4
        + [pltpu.SemaphoreType.DMA((8,)), pltpu.SemaphoreType.DMA((4,)), pltpu.SemaphoreType.DMA((4,))],
        compiler_params=pltpu.CompilerParams(
            collective_id=0, has_side_effects=True, vmem_limit_bytes=56 * 1024 * 1024
        ),
    )(velocity, *tables)


def solution(mesh):
    return jax.shard_map(
        local, mesh=mesh, in_specs=(P("wall", "space", None),), out_specs=P("wall", None, "space", None), check_vma=False
    )
```

```python
import math

import jax
import jax.numpy as jnp
import ml_dtypes
import numpy as np
from jax import lax
from jax.experimental import pallas as pl
from jax.experimental.pallas import tpu as pltpu
from jax.sharding import PartitionSpec as P

F32 = jnp.float32
BF16 = jnp.bfloat16
HALF = math.sqrt(0.5)

NX, NZ = 2048, 1024
SPREAD, ROWS = 32, 64
PEERS = 2 * SPREAD
TILE = 8
CHUNKS = 2
MESSAGE = TILE // CHUNKS
COLUMNS = MESSAGE // 2
RUN = COLUMNS * SPREAD


def split_table(table):
    high = table.astype(ml_dtypes.bfloat16)
    low = (table - high.astype(np.float64)).astype(ml_dtypes.bfloat16)
    return high, low


def mode_of(block, n):
    if block:
        return 8 * n + block
    return np.where(n < 64, 8 * n, 8 * (n - 64) + 4)


def slots():
    kb, dev, chunk, part, ka = np.meshgrid(*map(np.arange, (2, 16, CHUNKS, 2, COLUMNS)), indexing="ij")
    return dev * 8 + (chunk * COLUMNS + ka) * 2 + kb, part


def span_forward_tables():
    n, part = slots()
    n, part = n[..., None], part[..., None]
    zi = np.arange(128)
    out = np.zeros((4, 2, 128, 256))
    for block in range(4):
        angle = 2 * np.pi * (mode_of(block, n) * zi % NZ) / NZ
        cos, sin = np.cos(angle), np.sin(angle)
        from_re = np.where(part == 0, cos, -sin)
        from_im = np.where(part == 0, sin, cos)
        if block == 0:
            alternate = np.where(zi % 2 == 0, 1.0, -1.0)
            from_re = np.where((n == 0) & (part == 1), alternate, from_re)
            first = np.where(n < 64, from_re, 0.0)
            second = np.where(n < 64, 0.0, from_re)
        else:
            first, second = from_re, from_im
        out[block] = np.concatenate([first, second], axis=-1).reshape(2, 128, 256)
    high, low = split_table(out)
    return np.concatenate([high, low], axis=2)


def span_inverse_tables():
    n, part = slots()
    n, part = n[..., None], part[..., None]
    zi = np.arange(128)
    scale = (NX * NZ) ** -1.5
    out = np.zeros((4, 256, 256))
    for block in range(4):
        angle = 2 * np.pi * (mode_of(block, n) * zi % NZ) / NZ
        cos, sin = np.cos(angle), np.sin(angle)
        to_re = 2 * np.where(part == 0, cos, -sin)
        to_im = 2 * np.where(part == 0, sin, cos)
        if block == 0:
            alternate = np.where(zi % 2 == 0, 1.0, -1.0)
            to_re = np.where(n == 0, np.where(part == 0, 1.0, alternate), to_re)
            first = np.where(n < 64, to_re, 0.0)
            second = np.where(n < 64, 0.0, to_re)
        else:
            first, second = to_re, to_im
        out[block] = np.concatenate([first, second], axis=-1).reshape(256, 256) * scale
    high, low = split_table(out)
    return np.stack([high, low], axis=1)


def stream_outer_forward():
    out = np.zeros((2, RUN, SPREAD, TILE))
    mirror = np.zeros((2, SPREAD, SPREAD, TILE))
    t, s = np.arange(SPREAD)[:, None], np.arange(SPREAD)[None, :]
    cos, sin = np.cos(2 * np.pi * (t * s % 32) / 32), np.sin(2 * np.pi * (t * s % 32) / 32)
    for ka in range(COLUMNS):
        rows = slice(32 * ka, 32 * ka + 32)
        out[0, rows, :, ka] = cos
        out[0, rows, :, COLUMNS + ka] = sin
        out[1, rows, :, ka] = -sin
        out[1, rows, :, COLUMNS + ka] = cos
    mirror[0, :, :, 0] = cos
    mirror[0, :, :, COLUMNS] = -sin
    mirror[1, :, :, 0] = -sin
    mirror[1, :, :, COLUMNS] = -cos
    out = np.concatenate([out.reshape(2 * RUN, 256), mirror.reshape(64, 256)])
    return np.concatenate(split_table(out))


def stream_outer_inverse():
    out = np.zeros((SPREAD, 2, COLUMNS, 2, COLUMNS, SPREAD))
    s, t = np.arange(SPREAD)[:, None], np.arange(SPREAD)[None, :]
    cos, sin = np.cos(2 * np.pi * (t * s % 32) / 32), np.sin(2 * np.pi * (t * s % 32) / 32)
    for ka in range(COLUMNS):
        out[:, 0, ka, 0, ka] = cos
        out[:, 0, ka, 1, ka] = -sin
        out[:, 1, ka, 0, ka] = sin
        out[:, 1, ka, 1, ka] = cos
    high, low = split_table(out.reshape(2 * RUN, 2 * RUN))
    pad = np.zeros((2 * RUN, 128 - 2 * RUN), high.dtype)
    return np.concatenate([high, pad, low, pad], axis=1)


def stream_inner(sign):
    out = np.zeros((2, 2, ROWS, 2, 2, ROWS))
    r, m = np.arange(ROWS)[:, None], np.arange(ROWS)[None, :]
    cos, sin = np.cos(2 * np.pi * (r * m % 64) / 64), sign * np.sin(2 * np.pi * (r * m % 64) / 64)
    for kb in range(2):
        out[0, kb, :, 0, kb] = cos
        out[1, kb, :, 0, kb] = -sin
        out[0, kb, :, 1, kb] = sin
        out[1, kb, :, 1, kb] = cos
    return np.concatenate(split_table(out.reshape(256, 256)))


def twist_tables():
    angle = 2 * np.pi * np.outer(np.arange(SPREAD), np.tile(np.arange(ROWS), 2)) / NX
    return np.concatenate(split_table(np.concatenate([np.cos(angle), np.sin(angle)], axis=1)))


TABLES = {
    "span_forward": span_forward_tables().reshape(-1, 256),
    "outer_forward": stream_outer_forward(),
    "inner_forward": stream_inner(-1.0),
    "twist": twist_tables(),
    "inner_inverse": stream_inner(1.0),
    "outer_inverse": stream_outer_inverse(),
    "span_inverse": span_inverse_tables().reshape(-1, 256),
}
STARTS = dict(zip(TABLES, np.cumsum([0] + [t.shape[0] for t in TABLES.values()]).tolist()))
TABLE_ROWS = sum(t.shape[0] for t in TABLES.values())


def table_rows(tables, name, first, count):
    return tables[STARTS[name] + first : STARTS[name] + first + count, :]


def split(x):
    high = x.astype(BF16)
    return high, (x - high.astype(F32)).astype(BF16)


def mul(a, b):
    return jnp.dot(a, b, preferred_element_type=F32)


def mul_nt(a, b):
    return lax.dot_general(a, b, (((1,), (1,)), ((), ())), preferred_element_type=F32)


def stream_chunk(chunk, recv1, send2, tables, me_mode):
    used = lax.broadcasted_iota(jnp.int32, (256, 128), 0) % TILE < MESSAGE
    halves = [split(jnp.where(used, recv1[chunk, 256 * p : 256 * p + 256, :], 0.0)) for p in range(2)]
    extra = 64 if chunk == 0 else 0
    rows = RUN + extra // 2
    high, low = [table_rows(tables, "outer_forward", first, 2 * RUN + extra) for first in (0, 2 * RUN + 64)]
    outer = mul(high, jnp.concatenate([x for pair in halves for x in pair], axis=1))
    outer_low = mul(low, jnp.concatenate([x for x, _ in halves], axis=1))
    twist = table_rows(tables, "twist", 0, 32).astype(F32) + table_rows(tables, "twist", 32, 32).astype(F32)
    cos = jnp.concatenate([twist[:, :128]] * (rows // 32), axis=0)
    sin = jnp.concatenate([twist[:, 128:]] * (rows // 32), axis=0)
    turned = []
    for p in range(2):
        got = outer[:, 256 * p : 256 * p + 128] + outer[:, 256 * p + 128 : 256 * p + 256] + outer_low[:, 128 * p : 128 * p + 128]
        re, im = got[:RUN], got[RUN : 2 * RUN]
        if extra:
            re = jnp.concatenate([re, got[2 * RUN : 2 * RUN + 32]], axis=0)
            im = jnp.concatenate([im, got[2 * RUN + 32 :]], axis=0)
        turned.append(jnp.concatenate([re * cos + im * sin, im * cos - re * sin], axis=1))
    high, low = split(jnp.concatenate(turned, axis=0))
    both = mul(jnp.concatenate([high, low], axis=0), table_rows(tables, "inner_forward", 0, 256))
    spectra = both[: 2 * rows] + both[2 * rows :] + mul(high, table_rows(tables, "inner_forward", 256, 256))

    a_re, a_im = spectra[:RUN, :128], spectra[:RUN, 128:]
    b_re, b_im = spectra[rows : rows + RUN, :128], spectra[rows : rows + RUN, 128:]
    cross_re = a_re * b_re + a_im * b_im
    cross_im = a_re * b_im - a_im * b_re
    first, second = (cross_re, cross_im), (cross_re, -cross_im)

    if chunk == 0:
        def unpack(column, mirror):
            c_re, c_im = column[:, :128], column[:, 128:]
            m_re, m_im = mirror[:, :128], mirror[:, 128:]
            return (c_re + m_re) * 0.5, (c_im + m_im) * 0.5, (c_im - m_im) * 0.5, (m_re - c_re) * 0.5

        a0_re, a0_im, a1_re, a1_im = unpack(spectra[:32], spectra[RUN:rows])
        b0_re, b0_im, b1_re, b1_im = unpack(spectra[rows : rows + 32], spectra[rows + RUN :])
        zero_re, zero_im = a0_re * b0_re + a0_im * b0_im, a0_re * b0_im - a0_im * b0_re
        last_re, last_im = a1_re * b1_re + a1_im * b1_im, a1_re * b1_im - a1_im * b1_re
        lane = lax.broadcasted_iota(jnp.int32, (32, 128), 1)
        packed = jnp.logical_and(lane < ROWS, me_mode == 0)

        def merge(special, plain):
            head = jnp.where(packed, special, plain[:32])
            return head if RUN == 32 else jnp.concatenate([head, plain[32:]], axis=0)

        first = merge(zero_re - last_im, cross_re), merge(zero_im + last_re, cross_im)
        second = merge(zero_re + last_im, cross_re), merge(last_re - zero_im, -cross_im)

    high, low = split(jnp.concatenate([jnp.concatenate(first, axis=1), jnp.concatenate(second, axis=1)], axis=0))
    both = mul(jnp.concatenate([high, low], axis=0), table_rows(tables, "inner_inverse", 0, 256))
    inner = both[: 2 * RUN] + both[2 * RUN :] + mul(high, table_rows(tables, "inner_inverse", 256, 256))
    cos, sin = cos[:RUN], sin[:RUN]
    columns = []
    for p in range(2):
        re, im = inner[RUN * p : RUN * p + RUN, :128], inner[RUN * p : RUN * p + RUN, 128:]
        columns.append(split(jnp.concatenate([re * cos - im * sin, im * cos + re * sin], axis=0)))
    outer_table = table_rows(tables, "outer_inverse", 0, 2 * RUN)
    outer = mul(outer_table[:, : 2 * RUN], jnp.concatenate([x for pair in columns for x in pair], axis=1))
    outer_low = mul(outer_table[:, 128 : 128 + 2 * RUN], jnp.concatenate([x for x, _ in columns], axis=1))
    for p in range(2):
        got = outer[:, 256 * p : 256 * p + 128] + outer[:, 256 * p + 128 : 256 * p + 256] + outer_low[:, 128 * p : 128 * p + 128]
        got = got.reshape(SPREAD // CHUNKS, TILE, 128)
        spaced = jnp.stack([got] + [pltpu.roll(got, TILE - MESSAGE * i, 1) for i in range(1, CHUNKS)], axis=1)
        send2[chunk, 256 * p : 256 * p + 256, :] = spaced.reshape(256, 128)


def kernel(
    u_hbm, tables_hbm, out_ref, u, tables, e_high, e_low, send1, recv1, send2, recv2,
    load_sem, send_sem, recv_sem,
):
    wall, space = lax.axis_index("wall"), lax.axis_index("space")
    pairs = lax.axis_size("wall") // 2
    plane = wall // pairs
    base = lax.rem(wall, pairs)
    y, z = space // 8, lax.rem(space, 8)
    me_mode = y * 16 + plane * 8 + z
    me_row = plane * SPREAD + space

    first = STARTS["outer_forward"]
    loads = [
        pltpu.make_async_copy(u_hbm, u, load_sem.at[0]),
        pltpu.make_async_copy(tables_hbm.at[pl.ds(0, first)], tables.at[pl.ds(0, first)], load_sem.at[1]),
        pltpu.make_async_copy(
            tables_hbm.at[pl.ds(first, TABLE_ROWS - first)], tables.at[pl.ds(first, TABLE_ROWS - first)], load_sem.at[2]
        ),
    ]
    for load in loads:
        load.start()

    def address(to_plane, to_space):
        return {"device_id": {"wall": base + pairs * to_plane, "space": to_space}, "device_id_type": pl.DeviceIdType.MESH}

    def others(to_z, skip_self=False):
        for dy in (2, 3, 1, 0):
            for flip in (1, 0):
                if not (skip_self and flip == dy == 0):
                    yield lax.rem(plane + flip, 2), lax.rem(y + dy, 4) * 8 + to_z

    def everyone(act):
        @pl.loop(0, 7)
        def _(i):
            act(lax.rem(z + 4 + (1 - 2 * lax.rem(i, 2)) * ((i + 1) // 2), 8))

        act(z, skip_self=True)

    barrier = pltpu.get_barrier_semaphore()

    def greet(to_z, skip_self=False):
        for peer in others(to_z, skip_self):
            pl.semaphore_signal(barrier, inc=1, **address(*peer))

    everyone(greet)

    def tile(ref, index):
        return ref.at[pl.ds(pl.multiple_of(index * TILE, TILE), MESSAGE)]

    def exchange(stage, src, dst, place_there, place_here):
        def send(to_z, skip_self=False):
            for to_plane, to_space in others(to_z, skip_self):
                pltpu.make_async_remote_copy(
                    src_ref=tile(src, place_there(to_plane, to_space)), dst_ref=tile(dst, place_here),
                    send_sem=send_sem.at[stage], recv_sem=recv_sem.at[stage], **address(to_plane, to_space),
                ).start()

        everyone(send)
        pltpu.make_async_copy(tile(src, place_there(plane, space)), tile(dst, place_here), recv_sem.at[stage]).start()

    def wait_tiles(sem, count):
        rows = send1.at[0].at[pl.ds(0, count * MESSAGE)]
        pltpu.make_async_copy(rows, rows, sem).wait()

    def mode_place(of_plane, of_space):
        return (of_space // 8) * 16 + of_plane * 8 + lax.rem(of_space, 8)

    def row_place(of_plane, of_space):
        return of_plane * SPREAD + of_space

    loads[0].wait()
    parts = [u[0, :, 128 * b : 128 * b + 128] for b in range(8)]
    plus = [parts[b] + parts[b + 4] for b in range(4)]
    minus = [parts[b] - parts[b + 4] for b in range(4)]
    even, odd = plus[0] + plus[2], plus[1] + plus[3]
    across, along = (minus[1] - minus[3]) * HALF, (minus[1] + minus[3]) * HALF
    eighths = [
        (even + odd, even - odd),
        (minus[0] + across, -minus[2] - along),
        (plus[0] - plus[2], plus[3] - plus[1]),
        (minus[0] - across, minus[2] - along),
    ]
    for block, (first, second) in enumerate(eighths):
        for half, value in enumerate((first, second)):
            high, low = split(value)
            e_high[block, :, 128 * half : 128 * half + 128] = high
            e_low[block, :, 128 * half : 128 * half + 128] = low

    loads[1].wait()
    nothing = jnp.zeros((ROWS, 256), BF16)
    for block in range(4):
        high, low = e_high[block], e_low[block]
        first, second = [table_rows(tables, "span_forward", 512 * block + 256 * kb, 256) for kb in range(2)]
        both = mul_nt(first, jnp.concatenate([high, nothing, low, nothing], axis=0))
        both += mul_nt(second, jnp.concatenate([nothing, high, nothing, low], axis=0))
        got = both[:128, :128] + both[:128, 128:] + both[128:, :128]
        got = got.reshape(16, TILE, 128)
        for chunk in range(CHUNKS):
            turned = pltpu.roll(got, TILE - MESSAGE * chunk, 1) if chunk else got
            send1[chunk, 128 * block : 128 * block + 128, :] = turned.reshape(128, 128)

    pl.semaphore_wait(barrier, PEERS - 1)
    for chunk in range(CHUNKS):
        exchange(chunk, send1.at[chunk], recv1.at[chunk], mode_place, me_row)
    loads[2].wait()
    for chunk in range(CHUNKS):
        wait_tiles(recv_sem.at[chunk], PEERS)
        stream_chunk(chunk, recv1, send2, tables, me_mode)
        exchange(CHUNKS + chunk, send2.at[chunk], recv2.at[chunk], row_place, me_mode)
    for chunk in range(CHUNKS):
        wait_tiles(recv_sem.at[CHUNKS + chunk], PEERS)

    place = lax.broadcasted_iota(jnp.int32, (16, TILE, 128), 1) // MESSAGE
    fields = []
    for block in range(4):
        flat = recv2[0, 128 * block : 128 * block + 128, :].reshape(16, TILE, 128)
        for chunk in range(1, CHUNKS):
            got = recv2[chunk, 128 * block : 128 * block + 128, :].reshape(16, TILE, 128)
            flat = jnp.where(place == chunk, pltpu.roll(got, MESSAGE * chunk, 1), flat)
        flat = flat.reshape(128, 128).T
        high, low = split(jnp.concatenate([flat[:ROWS], flat[ROWS:]], axis=1))
        first, second = [table_rows(tables, "span_inverse", 512 * block + 256 * i, 256) for i in range(2)]
        both = mul(jnp.concatenate([high, low], axis=0), first)
        fields.append(both[:ROWS] + both[ROWS:] + mul(high, second))
    (h0, h4), (r1, i1), (r2, i2), (r3, i3) = [(f[:, :128], f[:, 128:]) for f in fields]
    sums, differences = h0 + h4, h0 - h4
    evens = [sums + r2, differences - i2, sums - r2, differences + i2]
    odds = [r1 + r3, (r1 - r3 - i1 - i3) * HALF, i3 - i1, (r3 - r1 - i1 - i3) * HALF]
    for b in range(4):
        out_ref[0, 0, :, 128 * b : 128 * b + 128] = evens[b] + odds[b]
        out_ref[0, 0, :, 128 * b + 512 : 128 * b + 640] = evens[b] - odds[b]

    for stage in range(2 * CHUNKS):
        wait_tiles(send_sem.at[stage], PEERS - 1)


def local(velocity):
    tables = jnp.asarray(np.concatenate(list(TABLES.values())))
    messages = pltpu.VMEM((CHUNKS, PEERS * TILE, 128), F32)
    return pl.pallas_call(
        kernel,
        out_shape=jax.ShapeDtypeStruct((1, 1, ROWS, NZ), F32),
        in_specs=[pl.BlockSpec(memory_space=pl.ANY)] * 2,
        out_specs=pl.BlockSpec(memory_space=pltpu.VMEM),
        scratch_shapes=[pltpu.VMEM(velocity.shape, F32), pltpu.VMEM(tables.shape, tables.dtype)]
        + [pltpu.VMEM((4, ROWS, 256), BF16)] * 2
        + [messages] * 4
        + [pltpu.SemaphoreType.DMA((n,)) for n in (3, 2 * CHUNKS, 2 * CHUNKS)],
        compiler_params=pltpu.CompilerParams(
            collective_id=0, has_side_effects=True, vmem_limit_bytes=107 * 512 * 1024
        ),
    )(velocity, tables)


def solution(mesh):
    return jax.shard_map(
        local, mesh=mesh, in_specs=(P("wall", "space", None),), out_specs=P("wall", None, "space", None), check_vma=False
    )
```

```python
import math

import jax
import jax.numpy as jnp
import ml_dtypes
import numpy as np
from jax import lax
from jax.experimental import pallas as pl
from jax.experimental.pallas import tpu as pltpu
from jax.sharding import PartitionSpec as P

F32 = jnp.float32
BF16 = jnp.bfloat16
HALF = math.sqrt(0.5)

NX, NZ = 2048, 1024
SPREAD, ROWS = 32, 64
PEERS = 2 * SPREAD
TILE = 8
CHUNKS = 2
MESSAGE = TILE // CHUNKS
COLUMNS = MESSAGE // 2
RUN = COLUMNS * SPREAD


def split_table(table):
    high = table.astype(ml_dtypes.bfloat16)
    low = (table - high.astype(np.float64)).astype(ml_dtypes.bfloat16)
    return high, low


def mode_of(block, n):
    if block:
        return 8 * n + block
    return np.where(n < 64, 8 * n, 8 * (n - 64) + 4)


def slots():
    kb, dev, chunk, part, ka = np.meshgrid(*map(np.arange, (2, 16, CHUNKS, 2, COLUMNS)), indexing="ij")
    return dev * 8 + (chunk * COLUMNS + ka) * 2 + kb, part


def span_forward_tables():
    n, part = slots()
    n, part = n[..., None], part[..., None]
    zi = np.arange(128)
    out = np.zeros((4, 2, 128, 256))
    for block in range(4):
        angle = 2 * np.pi * (mode_of(block, n) * zi % NZ) / NZ
        cos, sin = np.cos(angle), np.sin(angle)
        from_re = np.where(part == 0, cos, -sin)
        from_im = np.where(part == 0, sin, cos)
        if block == 0:
            alternate = np.where(zi % 2 == 0, 1.0, -1.0)
            from_re = np.where((n == 0) & (part == 1), alternate, from_re)
            first = np.where(n < 64, from_re, 0.0)
            second = np.where(n < 64, 0.0, from_re)
        else:
            first, second = from_re, from_im
        out[block] = np.concatenate([first, second], axis=-1).reshape(2, 128, 256)
    high, low = split_table(out)
    return np.concatenate([high, low], axis=2)


def span_inverse_tables():
    n, part = slots()
    n, part = n[..., None], part[..., None]
    zi = np.arange(128)
    scale = (NX * NZ) ** -1.5
    out = np.zeros((4, 256, 256))
    for block in range(4):
        angle = 2 * np.pi * (mode_of(block, n) * zi % NZ) / NZ
        cos, sin = np.cos(angle), np.sin(angle)
        to_re = 2 * np.where(part == 0, cos, -sin)
        to_im = 2 * np.where(part == 0, sin, cos)
        if block == 0:
            alternate = np.where(zi % 2 == 0, 1.0, -1.0)
            to_re = np.where(n == 0, np.where(part == 0, 1.0, alternate), to_re)
            first = np.where(n < 64, to_re, 0.0)
            second = np.where(n < 64, 0.0, to_re)
        else:
            first, second = to_re, to_im
        out[block] = np.concatenate([first, second], axis=-1).reshape(256, 256) * scale
    high, low = split_table(out)
    return np.stack([high, low], axis=1)


def stream_outer_forward():
    out = np.zeros((2, RUN, SPREAD, TILE))
    mirror = np.zeros((2, SPREAD, SPREAD, TILE))
    t, s = np.arange(SPREAD)[:, None], np.arange(SPREAD)[None, :]
    cos, sin = np.cos(2 * np.pi * (t * s % 32) / 32), np.sin(2 * np.pi * (t * s % 32) / 32)
    for ka in range(COLUMNS):
        rows = slice(32 * ka, 32 * ka + 32)
        out[0, rows, :, ka] = cos
        out[0, rows, :, COLUMNS + ka] = sin
        out[1, rows, :, ka] = -sin
        out[1, rows, :, COLUMNS + ka] = cos
    mirror[0, :, :, 0] = cos
    mirror[0, :, :, COLUMNS] = -sin
    mirror[1, :, :, 0] = -sin
    mirror[1, :, :, COLUMNS] = -cos
    out = np.concatenate([out.reshape(2 * RUN, 256), mirror.reshape(64, 256)])
    return np.concatenate(split_table(out))


def stream_outer_inverse():
    out = np.zeros((SPREAD, 2, COLUMNS, 2, COLUMNS, SPREAD))
    s, t = np.arange(SPREAD)[:, None], np.arange(SPREAD)[None, :]
    cos, sin = np.cos(2 * np.pi * (t * s % 32) / 32), np.sin(2 * np.pi * (t * s % 32) / 32)
    for ka in range(COLUMNS):
        out[:, 0, ka, 0, ka] = cos
        out[:, 0, ka, 1, ka] = -sin
        out[:, 1, ka, 0, ka] = sin
        out[:, 1, ka, 1, ka] = cos
    high, low = split_table(out.reshape(2 * RUN, 2 * RUN))
    pad = np.zeros((2 * RUN, 128 - 2 * RUN), high.dtype)
    return np.concatenate([high, pad, low, pad], axis=1)


def stream_inner(sign):
    out = np.zeros((2, 2, ROWS, 2, 2, ROWS))
    r, m = np.arange(ROWS)[:, None], np.arange(ROWS)[None, :]
    cos, sin = np.cos(2 * np.pi * (r * m % 64) / 64), sign * np.sin(2 * np.pi * (r * m % 64) / 64)
    for kb in range(2):
        out[0, kb, :, 0, kb] = cos
        out[1, kb, :, 0, kb] = -sin
        out[0, kb, :, 1, kb] = sin
        out[1, kb, :, 1, kb] = cos
    return np.concatenate(split_table(out.reshape(256, 256)))


def twist_tables():
    angle = 2 * np.pi * np.outer(np.arange(SPREAD), np.tile(np.arange(ROWS), 2)) / NX
    return np.concatenate(split_table(np.concatenate([np.cos(angle), np.sin(angle)], axis=1)))


TABLES = {
    "span_forward": span_forward_tables().reshape(-1, 256),
    "outer_forward": stream_outer_forward(),
    "inner_forward": stream_inner(-1.0),
    "twist": twist_tables(),
    "inner_inverse": stream_inner(1.0),
    "outer_inverse": stream_outer_inverse(),
    "span_inverse": span_inverse_tables().reshape(-1, 256),
}
STARTS = dict(zip(TABLES, np.cumsum([0] + [t.shape[0] for t in TABLES.values()]).tolist()))
TABLE_ROWS = sum(t.shape[0] for t in TABLES.values())


def table_rows(tables, name, first, count):
    return tables[STARTS[name] + first : STARTS[name] + first + count, :]


def split(x):
    high = x.astype(BF16)
    return high, (x - high.astype(F32)).astype(BF16)


def mul(a, b):
    return jnp.dot(a, b, preferred_element_type=F32)


def mul_nt(a, b):
    return lax.dot_general(a, b, (((1,), (1,)), ((), ())), preferred_element_type=F32)


def stream_chunk(chunk, recv1, send2, tables, me_mode):
    used = lax.broadcasted_iota(jnp.int32, (256, 128), 0) % TILE < MESSAGE
    halves = [split(jnp.where(used, recv1[chunk, 256 * p : 256 * p + 256, :], 0.0)) for p in range(2)]
    extra = 64 if chunk == 0 else 0
    rows = RUN + extra // 2
    high, low = [table_rows(tables, "outer_forward", first, 2 * RUN + extra) for first in (0, 2 * RUN + 64)]
    outer = mul(high, jnp.concatenate([x for pair in halves for x in pair], axis=1))
    outer_low = mul(low, jnp.concatenate([x for x, _ in halves], axis=1))
    twist = table_rows(tables, "twist", 0, 32).astype(F32) + table_rows(tables, "twist", 32, 32).astype(F32)
    cos = jnp.concatenate([twist[:, :128]] * (rows // 32), axis=0)
    sin = jnp.concatenate([twist[:, 128:]] * (rows // 32), axis=0)
    turned = []
    for p in range(2):
        got = outer[:, 256 * p : 256 * p + 128] + outer[:, 256 * p + 128 : 256 * p + 256] + outer_low[:, 128 * p : 128 * p + 128]
        re, im = got[:RUN], got[RUN : 2 * RUN]
        if extra:
            re = jnp.concatenate([re, got[2 * RUN : 2 * RUN + 32]], axis=0)
            im = jnp.concatenate([im, got[2 * RUN + 32 :]], axis=0)
        turned.append(jnp.concatenate([re * cos + im * sin, im * cos - re * sin], axis=1))
    high, low = split(jnp.concatenate(turned, axis=0))
    both = mul(jnp.concatenate([high, low], axis=0), table_rows(tables, "inner_forward", 0, 256))
    spectra = both[: 2 * rows] + both[2 * rows :] + mul(high, table_rows(tables, "inner_forward", 256, 256))

    a_re, a_im = spectra[:RUN, :128], spectra[:RUN, 128:]
    b_re, b_im = spectra[rows : rows + RUN, :128], spectra[rows : rows + RUN, 128:]
    cross_re = a_re * b_re + a_im * b_im
    cross_im = a_re * b_im - a_im * b_re
    first, second = (cross_re, cross_im), (cross_re, -cross_im)

    if chunk == 0:
        def unpack(column, mirror):
            c_re, c_im = column[:, :128], column[:, 128:]
            m_re, m_im = mirror[:, :128], mirror[:, 128:]
            return (c_re + m_re) * 0.5, (c_im + m_im) * 0.5, (c_im - m_im) * 0.5, (m_re - c_re) * 0.5

        a0_re, a0_im, a1_re, a1_im = unpack(spectra[:32], spectra[RUN:rows])
        b0_re, b0_im, b1_re, b1_im = unpack(spectra[rows : rows + 32], spectra[rows + RUN :])
        zero_re, zero_im = a0_re * b0_re + a0_im * b0_im, a0_re * b0_im - a0_im * b0_re
        last_re, last_im = a1_re * b1_re + a1_im * b1_im, a1_re * b1_im - a1_im * b1_re
        lane = lax.broadcasted_iota(jnp.int32, (32, 128), 1)
        packed = jnp.logical_and(lane < ROWS, me_mode == 0)

        def merge(special, plain):
            head = jnp.where(packed, special, plain[:32])
            return head if RUN == 32 else jnp.concatenate([head, plain[32:]], axis=0)

        first = merge(zero_re - last_im, cross_re), merge(zero_im + last_re, cross_im)
        second = merge(zero_re + last_im, cross_re), merge(last_re - zero_im, -cross_im)

    high, low = split(jnp.concatenate([jnp.concatenate(first, axis=1), jnp.concatenate(second, axis=1)], axis=0))
    both = mul(jnp.concatenate([high, low], axis=0), table_rows(tables, "inner_inverse", 0, 256))
    inner = both[: 2 * RUN] + both[2 * RUN :] + mul(high, table_rows(tables, "inner_inverse", 256, 256))
    cos, sin = cos[:RUN], sin[:RUN]
    columns = []
    for p in range(2):
        re, im = inner[RUN * p : RUN * p + RUN, :128], inner[RUN * p : RUN * p + RUN, 128:]
        columns.append(split(jnp.concatenate([re * cos - im * sin, im * cos + re * sin], axis=0)))
    outer_table = table_rows(tables, "outer_inverse", 0, 2 * RUN)
    outer = mul(outer_table[:, : 2 * RUN], jnp.concatenate([x for pair in columns for x in pair], axis=1))
    outer_low = mul(outer_table[:, 128 : 128 + 2 * RUN], jnp.concatenate([x for x, _ in columns], axis=1))
    for p in range(2):
        got = outer[:, 256 * p : 256 * p + 128] + outer[:, 256 * p + 128 : 256 * p + 256] + outer_low[:, 128 * p : 128 * p + 128]
        got = got.reshape(SPREAD // CHUNKS, TILE, 128)
        spaced = jnp.stack([got] + [pltpu.roll(got, TILE - MESSAGE * i, 1) for i in range(1, CHUNKS)], axis=1)
        send2[chunk, 256 * p : 256 * p + 256, :] = spaced.reshape(256, 128)


def kernel(
    u_hbm, tables_hbm, out_ref, u, tables, e_high, e_low, send1, recv1, send2, recv2,
    load_sem, send_sem, recv_sem,
):
    wall, space = lax.axis_index("wall"), lax.axis_index("space")
    pairs = lax.axis_size("wall") // 2
    plane = wall // pairs
    base = lax.rem(wall, pairs)
    y, z = space // 8, lax.rem(space, 8)
    me_mode = y * 16 + plane * 8 + z
    me_row = plane * SPREAD + space

    def address(to_plane, to_space):
        return {"device_id": {"wall": base + pairs * to_plane, "space": to_space}, "device_id_type": pl.DeviceIdType.MESH}

    def everyone(act):
        def row(flip, dz, steps):
            for dy in steps:
                act(lax.rem(plane + flip, 2), lax.rem(y + dy, 4) * 8 + lax.rem(z + dz, 8))

        for flip in (1, 0):
            @pl.loop(0, 7)
            def _(i):
                row(flip, 4 + (1 - 2 * lax.rem(i, 2)) * ((i + 1) // 2), (1, 3, 2, 0))

            row(flip, 0, (1, 3, 2, 0) if flip else (1, 3, 2))

    barrier = pltpu.get_barrier_semaphore()

    def greet(to_plane, to_space):
        pl.semaphore_signal(barrier, inc=1, **address(to_plane, to_space))

    everyone(greet)

    first = STARTS["outer_forward"]
    loads = [
        pltpu.make_async_copy(u_hbm, u, load_sem.at[0]),
        pltpu.make_async_copy(tables_hbm.at[pl.ds(0, first)], tables.at[pl.ds(0, first)], load_sem.at[1]),
        pltpu.make_async_copy(
            tables_hbm.at[pl.ds(first, TABLE_ROWS - first)], tables.at[pl.ds(first, TABLE_ROWS - first)], load_sem.at[2]
        ),
    ]
    for load in loads:
        load.start()

    def tile(ref, index):
        return ref.at[pl.ds(pl.multiple_of(index * TILE, TILE), MESSAGE)]

    def exchange(stage, src, dst, place_there, place_here):
        def send(to_plane, to_space):
            pltpu.make_async_remote_copy(
                src_ref=tile(src, place_there(to_plane, to_space)), dst_ref=tile(dst, place_here),
                send_sem=send_sem.at[stage], recv_sem=recv_sem.at[stage], **address(to_plane, to_space),
            ).start()

        everyone(send)
        pltpu.make_async_copy(tile(src, place_there(plane, space)), tile(dst, place_here), recv_sem.at[stage]).start()

    def wait_tiles(sem, count):
        rows = send1.at[0].at[pl.ds(0, count * MESSAGE)]
        pltpu.make_async_copy(rows, rows, sem).wait()

    def mode_place(of_plane, of_space):
        return (of_space // 8) * 16 + of_plane * 8 + lax.rem(of_space, 8)

    def row_place(of_plane, of_space):
        return of_plane * SPREAD + of_space

    loads[0].wait()
    parts = [u[0, :, 128 * b : 128 * b + 128] for b in range(8)]
    plus = [parts[b] + parts[b + 4] for b in range(4)]
    minus = [parts[b] - parts[b + 4] for b in range(4)]
    even, odd = plus[0] + plus[2], plus[1] + plus[3]
    across, along = (minus[1] - minus[3]) * HALF, (minus[1] + minus[3]) * HALF
    eighths = [
        (even + odd, even - odd),
        (minus[0] + across, -minus[2] - along),
        (plus[0] - plus[2], plus[3] - plus[1]),
        (minus[0] - across, minus[2] - along),
    ]
    for block, (first, second) in enumerate(eighths):
        for half, value in enumerate((first, second)):
            high, low = split(value)
            e_high[block, :, 128 * half : 128 * half + 128] = high
            e_low[block, :, 128 * half : 128 * half + 128] = low

    loads[1].wait()
    nothing = jnp.zeros((ROWS, 256), BF16)
    for block in range(4):
        high, low = e_high[block], e_low[block]
        first, second = [table_rows(tables, "span_forward", 512 * block + 256 * kb, 256) for kb in range(2)]
        both = mul_nt(first, jnp.concatenate([high, nothing, low, nothing], axis=0))
        both += mul_nt(second, jnp.concatenate([nothing, high, nothing, low], axis=0))
        got = both[:128, :128] + both[:128, 128:] + both[128:, :128]
        got = got.reshape(16, TILE, 128)
        for chunk in range(CHUNKS):
            turned = pltpu.roll(got, TILE - MESSAGE * chunk, 1) if chunk else got
            send1[chunk, 128 * block : 128 * block + 128, :] = turned.reshape(128, 128)

    pl.semaphore_wait(barrier, PEERS - 1)
    for chunk in range(CHUNKS):
        exchange(chunk, send1.at[chunk], recv1.at[chunk], mode_place, me_row)
    loads[2].wait()
    for chunk in range(CHUNKS):
        wait_tiles(recv_sem.at[chunk], PEERS)
        stream_chunk(chunk, recv1, send2, tables, me_mode)
        exchange(CHUNKS + chunk, send2.at[chunk], recv2.at[chunk], row_place, me_mode)
    for chunk in range(CHUNKS):
        wait_tiles(recv_sem.at[CHUNKS + chunk], PEERS)

    place = lax.broadcasted_iota(jnp.int32, (16, TILE, 128), 1) // MESSAGE
    fields = []
    for block in range(4):
        flat = recv2[0, 128 * block : 128 * block + 128, :].reshape(16, TILE, 128)
        for chunk in range(1, CHUNKS):
            got = recv2[chunk, 128 * block : 128 * block + 128, :].reshape(16, TILE, 128)
            flat = jnp.where(place == chunk, pltpu.roll(got, MESSAGE * chunk, 1), flat)
        flat = flat.reshape(128, 128).T
        high, low = split(jnp.concatenate([flat[:ROWS], flat[ROWS:]], axis=1))
        first, second = [table_rows(tables, "span_inverse", 512 * block + 256 * i, 256) for i in range(2)]
        both = mul(jnp.concatenate([high, low], axis=0), first)
        fields.append(both[:ROWS] + both[ROWS:] + mul(high, second))
    (h0, h4), (r1, i1), (r2, i2), (r3, i3) = [(f[:, :128], f[:, 128:]) for f in fields]
    sums, differences = h0 + h4, h0 - h4
    evens = [sums + r2, differences - i2, sums - r2, differences + i2]
    odds = [r1 + r3, (r1 - r3 - i1 - i3) * HALF, i3 - i1, (r3 - r1 - i1 - i3) * HALF]
    for b in range(4):
        out_ref[0, 0, :, 128 * b : 128 * b + 128] = evens[b] + odds[b]
        out_ref[0, 0, :, 128 * b + 512 : 128 * b + 640] = evens[b] - odds[b]

    for stage in range(2 * CHUNKS):
        wait_tiles(send_sem.at[stage], PEERS - 1)


def local(velocity):
    tables = jnp.asarray(np.concatenate(list(TABLES.values())))
    messages = pltpu.VMEM((CHUNKS, PEERS * TILE, 128), F32)
    return pl.pallas_call(
        kernel,
        out_shape=jax.ShapeDtypeStruct((1, 1, ROWS, NZ), F32),
        in_specs=[pl.BlockSpec(memory_space=pl.ANY)] * 2,
        out_specs=pl.BlockSpec(memory_space=pltpu.VMEM),
        scratch_shapes=[pltpu.VMEM(velocity.shape, F32), pltpu.VMEM(tables.shape, tables.dtype)]
        + [pltpu.VMEM((4, ROWS, 256), BF16)] * 2
        + [messages] * 4
        + [pltpu.SemaphoreType.DMA((n,)) for n in (3, 2 * CHUNKS, 2 * CHUNKS)],
        compiler_params=pltpu.CompilerParams(
            collective_id=0, has_side_effects=True, vmem_limit_bytes=107 * 512 * 1024
        ),
    )(velocity, tables)


def solution(mesh):
    return jax.shard_map(
        local, mesh=mesh, in_specs=(P("wall", "space", None),), out_specs=P("wall", None, "space", None), check_vma=False
    )
```

```python
import math

import jax
import jax.numpy as jnp
import ml_dtypes
import numpy as np
from jax import lax
from jax.experimental import pallas as pl
from jax.experimental.pallas import tpu as pltpu
from jax.sharding import PartitionSpec as P

F32 = jnp.float32
BF16 = jnp.bfloat16
HALF = math.sqrt(0.5)

NX, NZ = 2048, 1024
SPREAD, ROWS = 32, 64
PEERS = 2 * SPREAD
TILE = 8
CHUNKS = 2
MESSAGE = TILE // CHUNKS
COLUMNS = MESSAGE // 2
RUN = COLUMNS * SPREAD


def split_table(table):
    high = table.astype(ml_dtypes.bfloat16)
    low = (table - high.astype(np.float64)).astype(ml_dtypes.bfloat16)
    return high, low


def mode_of(block, n):
    if block:
        return 8 * n + block
    return np.where(n < 64, 8 * n, 8 * (n - 64) + 4)


def slots():
    kb, dev, chunk, part, ka = np.meshgrid(*map(np.arange, (2, 16, CHUNKS, 2, COLUMNS)), indexing="ij")
    return dev * 8 + (chunk * COLUMNS + ka) * 2 + kb, part


def span_forward_tables():
    n, part = slots()
    n, part = n[..., None], part[..., None]
    zi = np.arange(128)
    out = np.zeros((4, 2, 128, 256))
    for block in range(4):
        angle = 2 * np.pi * (mode_of(block, n) * zi % NZ) / NZ
        cos, sin = np.cos(angle), np.sin(angle)
        from_re = np.where(part == 0, cos, -sin)
        from_im = np.where(part == 0, sin, cos)
        if block == 0:
            alternate = np.where(zi % 2 == 0, 1.0, -1.0)
            from_re = np.where((n == 0) & (part == 1), alternate, from_re)
            first = np.where(n < 64, from_re, 0.0)
            second = np.where(n < 64, 0.0, from_re)
        else:
            first, second = from_re, from_im
        out[block] = np.concatenate([first, second], axis=-1).reshape(2, 128, 256)
    high, low = split_table(out)
    return np.concatenate([high, low], axis=2)


def span_inverse_tables():
    n, part = slots()
    n, part = n[..., None], part[..., None]
    zi = np.arange(128)
    scale = (NX * NZ) ** -1.5
    out = np.zeros((4, 256, 256))
    for block in range(4):
        angle = 2 * np.pi * (mode_of(block, n) * zi % NZ) / NZ
        cos, sin = np.cos(angle), np.sin(angle)
        to_re = 2 * np.where(part == 0, cos, -sin)
        to_im = 2 * np.where(part == 0, sin, cos)
        if block == 0:
            alternate = np.where(zi % 2 == 0, 1.0, -1.0)
            to_re = np.where(n == 0, np.where(part == 0, 1.0, alternate), to_re)
            first = np.where(n < 64, to_re, 0.0)
            second = np.where(n < 64, 0.0, to_re)
        else:
            first, second = to_re, to_im
        out[block] = np.concatenate([first, second], axis=-1).reshape(256, 256) * scale
    high, low = split_table(out)
    return np.stack([high, low], axis=1)


def stream_outer_forward():
    out = np.zeros((2, RUN, SPREAD, TILE))
    mirror = np.zeros((2, SPREAD, SPREAD, TILE))
    t, s = np.arange(SPREAD)[:, None], np.arange(SPREAD)[None, :]
    cos, sin = np.cos(2 * np.pi * (t * s % 32) / 32), np.sin(2 * np.pi * (t * s % 32) / 32)
    for ka in range(COLUMNS):
        rows = slice(32 * ka, 32 * ka + 32)
        out[0, rows, :, ka] = cos
        out[0, rows, :, COLUMNS + ka] = sin
        out[1, rows, :, ka] = -sin
        out[1, rows, :, COLUMNS + ka] = cos
    mirror[0, :, :, 0] = cos
    mirror[0, :, :, COLUMNS] = -sin
    mirror[1, :, :, 0] = -sin
    mirror[1, :, :, COLUMNS] = -cos
    out = np.concatenate([out.reshape(2 * RUN, 256), mirror.reshape(64, 256)])
    return np.concatenate(split_table(out))


def stream_outer_inverse():
    out = np.zeros((SPREAD, 2, COLUMNS, 2, COLUMNS, SPREAD))
    s, t = np.arange(SPREAD)[:, None], np.arange(SPREAD)[None, :]
    cos, sin = np.cos(2 * np.pi * (t * s % 32) / 32), np.sin(2 * np.pi * (t * s % 32) / 32)
    for ka in range(COLUMNS):
        out[:, 0, ka, 0, ka] = cos
        out[:, 0, ka, 1, ka] = -sin
        out[:, 1, ka, 0, ka] = sin
        out[:, 1, ka, 1, ka] = cos
    high, low = split_table(out.reshape(2 * RUN, 2 * RUN))
    pad = np.zeros((2 * RUN, 128 - 2 * RUN), high.dtype)
    return np.concatenate([high, pad, low, pad], axis=1)


def stream_inner(sign):
    out = np.zeros((2, 2, ROWS, 2, 2, ROWS))
    r, m = np.arange(ROWS)[:, None], np.arange(ROWS)[None, :]
    cos, sin = np.cos(2 * np.pi * (r * m % 64) / 64), sign * np.sin(2 * np.pi * (r * m % 64) / 64)
    for kb in range(2):
        out[0, kb, :, 0, kb] = cos
        out[1, kb, :, 0, kb] = -sin
        out[0, kb, :, 1, kb] = sin
        out[1, kb, :, 1, kb] = cos
    return np.concatenate(split_table(out.reshape(256, 256)))


def twist_tables():
    angle = 2 * np.pi * np.outer(np.arange(SPREAD), np.tile(np.arange(ROWS), 2)) / NX
    return np.concatenate(split_table(np.concatenate([np.cos(angle), np.sin(angle)], axis=1)))


TABLES = {
    "span_forward": span_forward_tables().reshape(-1, 256),
    "outer_forward": stream_outer_forward(),
    "inner_forward": stream_inner(-1.0),
    "twist": twist_tables(),
    "inner_inverse": stream_inner(1.0),
    "outer_inverse": stream_outer_inverse(),
    "span_inverse": span_inverse_tables().reshape(-1, 256),
}
STARTS = dict(zip(TABLES, np.cumsum([0] + [t.shape[0] for t in TABLES.values()]).tolist()))
TABLE_ROWS = sum(t.shape[0] for t in TABLES.values())


def table_rows(tables, name, first, count):
    return tables[STARTS[name] + first : STARTS[name] + first + count, :]


def split(x):
    high = x.astype(BF16)
    return high, (x - high.astype(F32)).astype(BF16)


def mul(a, b):
    return jnp.dot(a, b, preferred_element_type=F32)


def mul_nt(a, b):
    return lax.dot_general(a, b, (((1,), (1,)), ((), ())), preferred_element_type=F32)


def stream_chunk(chunk, recv1, send2, tables, me_mode):
    used = lax.broadcasted_iota(jnp.int32, (256, 128), 0) % TILE < MESSAGE
    halves = [split(jnp.where(used, recv1[chunk, 256 * p : 256 * p + 256, :], 0.0)) for p in range(2)]
    extra = 64 if chunk == 0 else 0
    rows = RUN + extra // 2
    high, low = [table_rows(tables, "outer_forward", first, 2 * RUN + extra) for first in (0, 2 * RUN + 64)]
    outer = mul(high, jnp.concatenate([x for pair in halves for x in pair], axis=1))
    outer_low = mul(low, jnp.concatenate([x for x, _ in halves], axis=1))
    twist = table_rows(tables, "twist", 0, 32).astype(F32) + table_rows(tables, "twist", 32, 32).astype(F32)
    cos = jnp.concatenate([twist[:, :128]] * (rows // 32), axis=0)
    sin = jnp.concatenate([twist[:, 128:]] * (rows // 32), axis=0)
    turned = []
    for p in range(2):
        got = outer[:, 256 * p : 256 * p + 128] + outer[:, 256 * p + 128 : 256 * p + 256] + outer_low[:, 128 * p : 128 * p + 128]
        re, im = got[:RUN], got[RUN : 2 * RUN]
        if extra:
            re = jnp.concatenate([re, got[2 * RUN : 2 * RUN + 32]], axis=0)
            im = jnp.concatenate([im, got[2 * RUN + 32 :]], axis=0)
        turned.append(jnp.concatenate([re * cos + im * sin, im * cos - re * sin], axis=1))
    high, low = split(jnp.concatenate(turned, axis=0))
    both = mul(jnp.concatenate([high, low], axis=0), table_rows(tables, "inner_forward", 0, 256))
    spectra = both[: 2 * rows] + both[2 * rows :] + mul(high, table_rows(tables, "inner_forward", 256, 256))

    a_re, a_im = spectra[:RUN, :128], spectra[:RUN, 128:]
    b_re, b_im = spectra[rows : rows + RUN, :128], spectra[rows : rows + RUN, 128:]
    cross_re = a_re * b_re + a_im * b_im
    cross_im = a_re * b_im - a_im * b_re
    first, second = (cross_re, cross_im), (cross_re, -cross_im)

    if chunk == 0:
        def unpack(column, mirror):
            c_re, c_im = column[:, :128], column[:, 128:]
            m_re, m_im = mirror[:, :128], mirror[:, 128:]
            return (c_re + m_re) * 0.5, (c_im + m_im) * 0.5, (c_im - m_im) * 0.5, (m_re - c_re) * 0.5

        a0_re, a0_im, a1_re, a1_im = unpack(spectra[:32], spectra[RUN:rows])
        b0_re, b0_im, b1_re, b1_im = unpack(spectra[rows : rows + 32], spectra[rows + RUN :])
        zero_re, zero_im = a0_re * b0_re + a0_im * b0_im, a0_re * b0_im - a0_im * b0_re
        last_re, last_im = a1_re * b1_re + a1_im * b1_im, a1_re * b1_im - a1_im * b1_re
        lane = lax.broadcasted_iota(jnp.int32, (32, 128), 1)
        packed = jnp.logical_and(lane < ROWS, me_mode == 0)

        def merge(special, plain):
            head = jnp.where(packed, special, plain[:32])
            return head if RUN == 32 else jnp.concatenate([head, plain[32:]], axis=0)

        first = merge(zero_re - last_im, cross_re), merge(zero_im + last_re, cross_im)
        second = merge(zero_re + last_im, cross_re), merge(last_re - zero_im, -cross_im)

    high, low = split(jnp.concatenate([jnp.concatenate(first, axis=1), jnp.concatenate(second, axis=1)], axis=0))
    both = mul(jnp.concatenate([high, low], axis=0), table_rows(tables, "inner_inverse", 0, 256))
    inner = both[: 2 * RUN] + both[2 * RUN :] + mul(high, table_rows(tables, "inner_inverse", 256, 256))
    cos, sin = cos[:RUN], sin[:RUN]
    columns = []
    for p in range(2):
        re, im = inner[RUN * p : RUN * p + RUN, :128], inner[RUN * p : RUN * p + RUN, 128:]
        columns.append(split(jnp.concatenate([re * cos - im * sin, im * cos + re * sin], axis=0)))
    outer_table = table_rows(tables, "outer_inverse", 0, 2 * RUN)
    outer = mul(outer_table[:, : 2 * RUN], jnp.concatenate([x for pair in columns for x in pair], axis=1))
    outer_low = mul(outer_table[:, 128 : 128 + 2 * RUN], jnp.concatenate([x for x, _ in columns], axis=1))
    for p in range(2):
        got = outer[:, 256 * p : 256 * p + 128] + outer[:, 256 * p + 128 : 256 * p + 256] + outer_low[:, 128 * p : 128 * p + 128]
        got = got.reshape(SPREAD // CHUNKS, TILE, 128)
        spaced = jnp.stack([got] + [pltpu.roll(got, TILE - MESSAGE * i, 1) for i in range(1, CHUNKS)], axis=1)
        send2[chunk, 256 * p : 256 * p + 256, :] = spaced.reshape(256, 128)


def kernel(
    u_hbm, tables_hbm, out_ref, u, tables, e_high, e_low, send1, recv1, send2, recv2,
    load_sem, send_sem, recv_sem,
):
    wall, space = lax.axis_index("wall"), lax.axis_index("space")
    pairs = lax.axis_size("wall") // 2
    plane = wall // pairs
    base = lax.rem(wall, pairs)
    y, z = space // 8, lax.rem(space, 8)
    me_mode = y * 16 + plane * 8 + z
    me_row = plane * SPREAD + space

    def address(to_plane, to_space):
        return {"device_id": {"wall": base + pairs * to_plane, "space": to_space}, "device_id_type": pl.DeviceIdType.MESH}

    def everyone(act):
        def row(flip, steps, *shifts):
            for dy in steps:
                for dz in shifts:
                    act(lax.rem(plane + flip, 2), lax.rem(y + dy, 4) * 8 + lax.rem(z + dz, 8))

        for flip in (1, 0):
            row(flip, (1, 3, 2, 0), 4)

            @pl.loop(1, 4)
            def _(i):
                row(flip, (1, 3, 2, 0), 4 - i, 4 + i)

            row(flip, (1, 3, 2, 0) if flip else (1, 3, 2), 0)

    barrier = pltpu.get_barrier_semaphore()

    def greet(to_plane, to_space):
        pl.semaphore_signal(barrier, inc=1, **address(to_plane, to_space))

    everyone(greet)

    first = STARTS["outer_forward"]
    loads = [
        pltpu.make_async_copy(u_hbm, u, load_sem.at[0]),
        pltpu.make_async_copy(tables_hbm.at[pl.ds(0, first)], tables.at[pl.ds(0, first)], load_sem.at[1]),
        pltpu.make_async_copy(
            tables_hbm.at[pl.ds(first, TABLE_ROWS - first)], tables.at[pl.ds(first, TABLE_ROWS - first)], load_sem.at[2]
        ),
    ]
    for load in loads:
        load.start()

    def tile(ref, index):
        return ref.at[pl.ds(pl.multiple_of(index * TILE, TILE), MESSAGE)]

    def exchange(stage, src, dst, place_there, place_here):
        def send(to_plane, to_space):
            pltpu.make_async_remote_copy(
                src_ref=tile(src, place_there(to_plane, to_space)), dst_ref=tile(dst, place_here),
                send_sem=send_sem.at[stage], recv_sem=recv_sem.at[stage], **address(to_plane, to_space),
            ).start()

        everyone(send)
        pltpu.make_async_copy(tile(src, place_there(plane, space)), tile(dst, place_here), recv_sem.at[stage]).start()

    def wait_tiles(sem, count):
        rows = send1.at[0].at[pl.ds(0, count * MESSAGE)]
        pltpu.make_async_copy(rows, rows, sem).wait()

    def mode_place(of_plane, of_space):
        return (of_space // 8) * 16 + of_plane * 8 + lax.rem(of_space, 8)

    def row_place(of_plane, of_space):
        return of_plane * SPREAD + of_space

    loads[0].wait()
    parts = [u[0, :, 128 * b : 128 * b + 128] for b in range(8)]
    plus = [parts[b] + parts[b + 4] for b in range(4)]
    minus = [parts[b] - parts[b + 4] for b in range(4)]
    even, odd = plus[0] + plus[2], plus[1] + plus[3]
    across, along = (minus[1] - minus[3]) * HALF, (minus[1] + minus[3]) * HALF
    eighths = [
        (even + odd, even - odd),
        (minus[0] + across, -minus[2] - along),
        (plus[0] - plus[2], plus[3] - plus[1]),
        (minus[0] - across, minus[2] - along),
    ]
    for block, (first, second) in enumerate(eighths):
        for half, value in enumerate((first, second)):
            high, low = split(value)
            e_high[block, :, 128 * half : 128 * half + 128] = high
            e_low[block, :, 128 * half : 128 * half + 128] = low

    loads[1].wait()
    nothing = jnp.zeros((ROWS, 256), BF16)
    @pl.loop(0, 4)
    def _(block):
        high, low = e_high[block], e_low[block]
        first, second = [tables[pl.ds(pl.multiple_of(512 * block + 256 * kb, 256), 256), :] for kb in range(2)]
        both = mul_nt(first, jnp.concatenate([high, nothing, low, nothing], axis=0))
        both += mul_nt(second, jnp.concatenate([nothing, high, nothing, low], axis=0))
        got = both[:128, :128] + both[:128, 128:] + both[128:, :128]
        got = got.reshape(16, TILE, 128)
        for chunk in range(CHUNKS):
            turned = pltpu.roll(got, TILE - MESSAGE * chunk, 1) if chunk else got
            send1[chunk, pl.ds(pl.multiple_of(128 * block, 128), 128), :] = turned.reshape(128, 128)

    pl.semaphore_wait(barrier, PEERS - 1)
    for chunk in range(CHUNKS):
        exchange(chunk, send1.at[chunk], recv1.at[chunk], mode_place, me_row)
    loads[2].wait()
    for chunk in range(CHUNKS):
        wait_tiles(recv_sem.at[chunk], PEERS)
        stream_chunk(chunk, recv1, send2, tables, me_mode)
        exchange(CHUNKS + chunk, send2.at[chunk], recv2.at[chunk], row_place, me_mode)
    for chunk in range(CHUNKS):
        wait_tiles(recv_sem.at[CHUNKS + chunk], PEERS)

    place = lax.broadcasted_iota(jnp.int32, (16, TILE, 128), 1) // MESSAGE
    fields = []
    for block in range(4):
        flat = recv2[0, 128 * block : 128 * block + 128, :].reshape(16, TILE, 128)
        for chunk in range(1, CHUNKS):
            got = recv2[chunk, 128 * block : 128 * block + 128, :].reshape(16, TILE, 128)
            flat = jnp.where(place == chunk, pltpu.roll(got, MESSAGE * chunk, 1), flat)
        flat = flat.reshape(128, 128).T
        high, low = split(jnp.concatenate([flat[:ROWS], flat[ROWS:]], axis=1))
        first, second = [table_rows(tables, "span_inverse", 512 * block + 256 * i, 256) for i in range(2)]
        both = mul(jnp.concatenate([high, low], axis=0), first)
        fields.append(both[:ROWS] + both[ROWS:] + mul(high, second))
    (h0, h4), (r1, i1), (r2, i2), (r3, i3) = [(f[:, :128], f[:, 128:]) for f in fields]
    sums, differences = h0 + h4, h0 - h4
    evens = [sums + r2, differences - i2, sums - r2, differences + i2]
    odds = [r1 + r3, (r1 - r3 - i1 - i3) * HALF, i3 - i1, (r3 - r1 - i1 - i3) * HALF]
    for b in range(4):
        out_ref[0, 0, :, 128 * b : 128 * b + 128] = evens[b] + odds[b]
        out_ref[0, 0, :, 128 * b + 512 : 128 * b + 640] = evens[b] - odds[b]

    for stage in range(2 * CHUNKS):
        wait_tiles(send_sem.at[stage], PEERS - 1)


def local(velocity):
    tables = jnp.asarray(np.concatenate(list(TABLES.values())))
    messages = pltpu.VMEM((CHUNKS, PEERS * TILE, 128), F32)
    return pl.pallas_call(
        kernel,
        out_shape=jax.ShapeDtypeStruct((1, 1, ROWS, NZ), F32),
        in_specs=[pl.BlockSpec(memory_space=pl.ANY)] * 2,
        out_specs=pl.BlockSpec(memory_space=pltpu.VMEM),
        scratch_shapes=[pltpu.VMEM(velocity.shape, F32), pltpu.VMEM(tables.shape, tables.dtype)]
        + [pltpu.VMEM((4, ROWS, 256), BF16)] * 2
        + [messages] * 4
        + [pltpu.SemaphoreType.DMA((n,)) for n in (3, 2 * CHUNKS, 2 * CHUNKS)],
        compiler_params=pltpu.CompilerParams(
            collective_id=0, has_side_effects=True, vmem_limit_bytes=107 * 512 * 1024
        ),
    )(velocity, tables)


def solution(mesh):
    return jax.shard_map(
        local, mesh=mesh, in_specs=(P("wall", "space", None),), out_specs=P("wall", None, "space", None), check_vma=False
    )
```

```python
import math

import jax
import jax.numpy as jnp
import ml_dtypes
import numpy as np
from jax import lax
from jax.experimental import pallas as pl
from jax.experimental.pallas import tpu as pltpu
from jax.sharding import PartitionSpec as P

F32 = jnp.float32
BF16 = jnp.bfloat16
HALF = math.sqrt(0.5)

NX, NZ = 2048, 1024
SPREAD, ROWS = 32, 64
PEERS = 2 * SPREAD
TILE = 8
CHUNKS = 2
MESSAGE = TILE // CHUNKS
COLUMNS = MESSAGE // 2
RUN = COLUMNS * SPREAD


def split_table(table):
    high = table.astype(ml_dtypes.bfloat16)
    low = (table - high.astype(np.float64)).astype(ml_dtypes.bfloat16)
    return high, low


def mode_of(block, n):
    if block:
        return 8 * n + block
    return np.where(n < 64, 8 * n, 8 * (n - 64) + 4)


def slots():
    kb, dev, chunk, part, ka = np.meshgrid(*map(np.arange, (2, 16, CHUNKS, 2, COLUMNS)), indexing="ij")
    return dev * 8 + (chunk * COLUMNS + ka) * 2 + kb, part


def span_forward_tables():
    n, part = slots()
    n, part = n[..., None], part[..., None]
    zi = np.arange(128)
    out = np.zeros((4, 2, 128, 256))
    for block in range(4):
        angle = 2 * np.pi * (mode_of(block, n) * zi % NZ) / NZ
        cos, sin = np.cos(angle), np.sin(angle)
        from_re = np.where(part == 0, cos, -sin)
        from_im = np.where(part == 0, sin, cos)
        if block == 0:
            alternate = np.where(zi % 2 == 0, 1.0, -1.0)
            from_re = np.where((n == 0) & (part == 1), alternate, from_re)
            first = np.where(n < 64, from_re, 0.0)
            second = np.where(n < 64, 0.0, from_re)
        else:
            first, second = from_re, from_im
        out[block] = np.concatenate([first, second], axis=-1).reshape(2, 128, 256)
    high, low = split_table(out)
    return np.concatenate([high, low], axis=2)


def span_inverse_tables():
    n, part = slots()
    n, part = n[..., None], part[..., None]
    zi = np.arange(128)
    scale = (NX * NZ) ** -1.5
    out = np.zeros((4, 256, 256))
    for block in range(4):
        angle = 2 * np.pi * (mode_of(block, n) * zi % NZ) / NZ
        cos, sin = np.cos(angle), np.sin(angle)
        to_re = 2 * np.where(part == 0, cos, -sin)
        to_im = 2 * np.where(part == 0, sin, cos)
        if block == 0:
            alternate = np.where(zi % 2 == 0, 1.0, -1.0)
            to_re = np.where(n == 0, np.where(part == 0, 1.0, alternate), to_re)
            first = np.where(n < 64, to_re, 0.0)
            second = np.where(n < 64, 0.0, to_re)
        else:
            first, second = to_re, to_im
        out[block] = np.concatenate([first, second], axis=-1).reshape(256, 256) * scale
    high, low = split_table(out)
    return np.stack([high, low], axis=1)


def stream_outer_forward():
    out = np.zeros((2, RUN, SPREAD, TILE))
    mirror = np.zeros((2, SPREAD, SPREAD, TILE))
    t, s = np.arange(SPREAD)[:, None], np.arange(SPREAD)[None, :]
    cos, sin = np.cos(2 * np.pi * (t * s % 32) / 32), np.sin(2 * np.pi * (t * s % 32) / 32)
    for ka in range(COLUMNS):
        rows = slice(32 * ka, 32 * ka + 32)
        out[0, rows, :, ka] = cos
        out[0, rows, :, COLUMNS + ka] = sin
        out[1, rows, :, ka] = -sin
        out[1, rows, :, COLUMNS + ka] = cos
    mirror[0, :, :, 0] = cos
    mirror[0, :, :, COLUMNS] = -sin
    mirror[1, :, :, 0] = -sin
    mirror[1, :, :, COLUMNS] = -cos
    out = np.concatenate([out.reshape(2 * RUN, 256), mirror.reshape(64, 256)])
    return np.concatenate(split_table(out))


def stream_outer_inverse():
    out = np.zeros((SPREAD, 2, COLUMNS, 2, COLUMNS, SPREAD))
    s, t = np.arange(SPREAD)[:, None], np.arange(SPREAD)[None, :]
    cos, sin = np.cos(2 * np.pi * (t * s % 32) / 32), np.sin(2 * np.pi * (t * s % 32) / 32)
    for ka in range(COLUMNS):
        out[:, 0, ka, 0, ka] = cos
        out[:, 0, ka, 1, ka] = -sin
        out[:, 1, ka, 0, ka] = sin
        out[:, 1, ka, 1, ka] = cos
    high, low = split_table(out.reshape(2 * RUN, 2 * RUN))
    pad = np.zeros((2 * RUN, 128 - 2 * RUN), high.dtype)
    return np.concatenate([high, pad, low, pad], axis=1)


def stream_inner(sign):
    out = np.zeros((2, 2, ROWS, 2, 2, ROWS))
    r, m = np.arange(ROWS)[:, None], np.arange(ROWS)[None, :]
    cos, sin = np.cos(2 * np.pi * (r * m % 64) / 64), sign * np.sin(2 * np.pi * (r * m % 64) / 64)
    for kb in range(2):
        out[0, kb, :, 0, kb] = cos
        out[1, kb, :, 0, kb] = -sin
        out[0, kb, :, 1, kb] = sin
        out[1, kb, :, 1, kb] = cos
    return np.concatenate(split_table(out.reshape(256, 256)))


def twist_tables():
    angle = 2 * np.pi * np.outer(np.arange(SPREAD), np.tile(np.arange(ROWS), 2)) / NX
    return np.concatenate(split_table(np.concatenate([np.cos(angle), np.sin(angle)], axis=1)))


TABLES = {
    "span_forward": span_forward_tables().reshape(-1, 256),
    "outer_forward": stream_outer_forward(),
    "inner_forward": stream_inner(-1.0),
    "twist": twist_tables(),
    "inner_inverse": stream_inner(1.0),
    "outer_inverse": stream_outer_inverse(),
    "span_inverse": span_inverse_tables().reshape(-1, 256),
}
STARTS = dict(zip(TABLES, np.cumsum([0] + [t.shape[0] for t in TABLES.values()]).tolist()))
TABLE_ROWS = sum(t.shape[0] for t in TABLES.values())


def table_rows(tables, name, first, count):
    return tables[STARTS[name] + first : STARTS[name] + first + count, :]


def split(x):
    high = x.astype(BF16)
    return high, (x - high.astype(F32)).astype(BF16)


def mul(a, b):
    return jnp.dot(a, b, preferred_element_type=F32)


def mul_nt(a, b):
    return lax.dot_general(a, b, (((1,), (1,)), ((), ())), preferred_element_type=F32)


def stream_chunk(chunk, recv1, send2, tables, me_mode):
    used = lax.broadcasted_iota(jnp.int32, (256, 128), 0) % TILE < MESSAGE
    halves = [split(jnp.where(used, recv1[chunk, 256 * p : 256 * p + 256, :], 0.0)) for p in range(2)]
    extra = 64 if chunk == 0 else 0
    rows = RUN + extra // 2
    high, low = [table_rows(tables, "outer_forward", first, 2 * RUN + extra) for first in (0, 2 * RUN + 64)]
    outer = mul(high, jnp.concatenate([x for pair in halves for x in pair], axis=1))
    outer_low = mul(low, jnp.concatenate([x for x, _ in halves], axis=1))
    twist = table_rows(tables, "twist", 0, 32).astype(F32) + table_rows(tables, "twist", 32, 32).astype(F32)
    cos = jnp.concatenate([twist[:, :128]] * (rows // 32), axis=0)
    sin = jnp.concatenate([twist[:, 128:]] * (rows // 32), axis=0)
    turned = []
    for p in range(2):
        got = outer[:, 256 * p : 256 * p + 128] + outer[:, 256 * p + 128 : 256 * p + 256] + outer_low[:, 128 * p : 128 * p + 128]
        re, im = got[:RUN], got[RUN : 2 * RUN]
        if extra:
            re = jnp.concatenate([re, got[2 * RUN : 2 * RUN + 32]], axis=0)
            im = jnp.concatenate([im, got[2 * RUN + 32 :]], axis=0)
        turned.append(jnp.concatenate([re * cos + im * sin, im * cos - re * sin], axis=1))
    high, low = split(jnp.concatenate(turned, axis=0))
    both = mul(jnp.concatenate([high, low], axis=0), table_rows(tables, "inner_forward", 0, 256))
    spectra = both[: 2 * rows] + both[2 * rows :] + mul(high, table_rows(tables, "inner_forward", 256, 256))

    a_re, a_im = spectra[:RUN, :128], spectra[:RUN, 128:]
    b_re, b_im = spectra[rows : rows + RUN, :128], spectra[rows : rows + RUN, 128:]
    cross_re = a_re * b_re + a_im * b_im
    cross_im = a_re * b_im - a_im * b_re
    first, second = (cross_re, cross_im), (cross_re, -cross_im)

    if chunk == 0:
        def unpack(column, mirror):
            c_re, c_im = column[:, :128], column[:, 128:]
            m_re, m_im = mirror[:, :128], mirror[:, 128:]
            return (c_re + m_re) * 0.5, (c_im + m_im) * 0.5, (c_im - m_im) * 0.5, (m_re - c_re) * 0.5

        a0_re, a0_im, a1_re, a1_im = unpack(spectra[:32], spectra[RUN:rows])
        b0_re, b0_im, b1_re, b1_im = unpack(spectra[rows : rows + 32], spectra[rows + RUN :])
        zero_re, zero_im = a0_re * b0_re + a0_im * b0_im, a0_re * b0_im - a0_im * b0_re
        last_re, last_im = a1_re * b1_re + a1_im * b1_im, a1_re * b1_im - a1_im * b1_re
        lane = lax.broadcasted_iota(jnp.int32, (32, 128), 1)
        packed = jnp.logical_and(lane < ROWS, me_mode == 0)

        def merge(special, plain):
            head = jnp.where(packed, special, plain[:32])
            return head if RUN == 32 else jnp.concatenate([head, plain[32:]], axis=0)

        first = merge(zero_re - last_im, cross_re), merge(zero_im + last_re, cross_im)
        second = merge(zero_re + last_im, cross_re), merge(last_re - zero_im, -cross_im)

    high, low = split(jnp.concatenate([jnp.concatenate(first, axis=1), jnp.concatenate(second, axis=1)], axis=0))
    both = mul(jnp.concatenate([high, low], axis=0), table_rows(tables, "inner_inverse", 0, 256))
    inner = both[: 2 * RUN] + both[2 * RUN :] + mul(high, table_rows(tables, "inner_inverse", 256, 256))
    cos, sin = cos[:RUN], sin[:RUN]
    columns = []
    for p in range(2):
        re, im = inner[RUN * p : RUN * p + RUN, :128], inner[RUN * p : RUN * p + RUN, 128:]
        columns.append(split(jnp.concatenate([re * cos - im * sin, im * cos + re * sin], axis=0)))
    outer_table = table_rows(tables, "outer_inverse", 0, 2 * RUN)
    outer = mul(outer_table[:, : 2 * RUN], jnp.concatenate([x for pair in columns for x in pair], axis=1))
    outer_low = mul(outer_table[:, 128 : 128 + 2 * RUN], jnp.concatenate([x for x, _ in columns], axis=1))
    for p in range(2):
        got = outer[:, 256 * p : 256 * p + 128] + outer[:, 256 * p + 128 : 256 * p + 256] + outer_low[:, 128 * p : 128 * p + 128]
        got = got.reshape(SPREAD // CHUNKS, TILE, 128)
        spaced = jnp.stack([got] + [pltpu.roll(got, TILE - MESSAGE * i, 1) for i in range(1, CHUNKS)], axis=1)
        send2[chunk, 256 * p : 256 * p + 256, :] = spaced.reshape(256, 128)


def kernel(
    u_hbm, tables_hbm, out_ref, u, tables, e_high, e_low, send1, recv1, send2, recv2,
    load_sem, send_sem, recv_sem,
):
    wall, space = lax.axis_index("wall"), lax.axis_index("space")
    pairs = lax.axis_size("wall") // 2
    plane = wall // pairs
    base = lax.rem(wall, pairs)
    y, z = space // 8, lax.rem(space, 8)
    me_mode = y * 16 + plane * 8 + z
    me_row = plane * SPREAD + space

    def address(to_plane, to_space):
        return {"device_id": {"wall": base + pairs * to_plane, "space": to_space}, "device_id_type": pl.DeviceIdType.MESH}

    def everyone(act):
        def row(flip, steps, *shifts):
            for dy in steps:
                for dz in shifts:
                    act(lax.rem(plane + flip, 2), lax.rem(y + dy, 4) * 8 + lax.rem(z + dz, 8))

        for flip in (1, 0):
            row(flip, (1, 3, 2, 0), 4)

            @pl.loop(1, 4)
            def _(i):
                row(flip, (1, 3, 2, 0), 4 - i, 4 + i)

            row(flip, (1, 3, 2, 0) if flip else (1, 3, 2), 0)

    barrier = pltpu.get_barrier_semaphore()

    def greet(to_plane, to_space):
        pl.semaphore_signal(barrier, inc=1, **address(to_plane, to_space))

    everyone(greet)

    first = STARTS["outer_forward"]
    loads = [
        pltpu.make_async_copy(u_hbm, u, load_sem.at[0]),
        pltpu.make_async_copy(tables_hbm.at[pl.ds(0, first)], tables.at[pl.ds(0, first)], load_sem.at[1]),
        pltpu.make_async_copy(
            tables_hbm.at[pl.ds(first, TABLE_ROWS - first)], tables.at[pl.ds(first, TABLE_ROWS - first)], load_sem.at[2]
        ),
    ]
    for load in loads:
        load.start()

    def tile(ref, index):
        return ref.at[pl.ds(pl.multiple_of(index * TILE, TILE), MESSAGE)]

    def exchange(stage, src, dst, place_there, place_here):
        def send(to_plane, to_space):
            pltpu.make_async_remote_copy(
                src_ref=tile(src, place_there(to_plane, to_space)), dst_ref=tile(dst, place_here),
                send_sem=send_sem.at[stage], recv_sem=recv_sem.at[stage], **address(to_plane, to_space),
            ).start()

        everyone(send)
        pltpu.make_async_copy(tile(src, place_there(plane, space)), tile(dst, place_here), recv_sem.at[stage]).start()

    def wait_tiles(sem, count):
        rows = send1.at[0].at[pl.ds(0, count * MESSAGE)]
        pltpu.make_async_copy(rows, rows, sem).wait()

    def mode_place(of_plane, of_space):
        return (of_space // 8) * 16 + of_plane * 8 + lax.rem(of_space, 8)

    def row_place(of_plane, of_space):
        return of_plane * SPREAD + of_space

    loads[0].wait()
    parts = [u[0, :, 128 * b : 128 * b + 128] for b in range(8)]
    plus = [parts[b] + parts[b + 4] for b in range(4)]
    minus = [parts[b] - parts[b + 4] for b in range(4)]
    even, odd = plus[0] + plus[2], plus[1] + plus[3]
    across, along = (minus[1] - minus[3]) * HALF, (minus[1] + minus[3]) * HALF
    eighths = [
        (even + odd, even - odd),
        (minus[0] + across, -minus[2] - along),
        (plus[0] - plus[2], plus[3] - plus[1]),
        (minus[0] - across, minus[2] - along),
    ]
    for block, (first, second) in enumerate(eighths):
        for half, value in enumerate((first, second)):
            high, low = split(value)
            e_high[block, :, 128 * half : 128 * half + 128] = high
            e_low[block, :, 128 * half : 128 * half + 128] = low

    loads[1].wait()
    nothing = jnp.zeros((ROWS, 256), BF16)
    @pl.loop(0, 4)
    def _(block):
        high, low = e_high[block], e_low[block]
        first, second = [tables[pl.ds(pl.multiple_of(512 * block + 256 * kb, 256), 256), :] for kb in range(2)]
        both = mul_nt(first, jnp.concatenate([high, nothing, low, nothing], axis=0))
        both += mul_nt(second, jnp.concatenate([nothing, high, nothing, low], axis=0))
        got = both[:128, :128] + both[:128, 128:] + both[128:, :128]
        got = got.reshape(16, TILE, 128)
        for chunk in range(CHUNKS):
            turned = pltpu.roll(got, TILE - MESSAGE * chunk, 1) if chunk else got
            send1[chunk, pl.ds(pl.multiple_of(128 * block, 128), 128), :] = turned.reshape(128, 128)

    pl.semaphore_wait(barrier, PEERS - 1)
    for chunk in range(CHUNKS):
        exchange(chunk, send1.at[chunk], recv1.at[chunk], mode_place, me_row)
    loads[2].wait()
    for chunk in range(CHUNKS):
        wait_tiles(recv_sem.at[chunk], PEERS)
        stream_chunk(chunk, recv1, send2, tables, me_mode)
        exchange(CHUNKS + chunk, send2.at[chunk], recv2.at[chunk], row_place, me_mode)
    for stage in range(2 * CHUNKS):
        wait_tiles(send_sem.at[stage], PEERS - 1)
    for chunk in range(CHUNKS):
        wait_tiles(recv_sem.at[CHUNKS + chunk], PEERS)

    place = lax.broadcasted_iota(jnp.int32, (16, TILE, 128), 1) // MESSAGE
    fields = []
    for block in range(4):
        flat = recv2[0, 128 * block : 128 * block + 128, :].reshape(16, TILE, 128)
        for chunk in range(1, CHUNKS):
            got = recv2[chunk, 128 * block : 128 * block + 128, :].reshape(16, TILE, 128)
            flat = jnp.where(place == chunk, pltpu.roll(got, MESSAGE * chunk, 1), flat)
        flat = flat.reshape(128, 128).T
        high, low = split(jnp.concatenate([flat[:ROWS], flat[ROWS:]], axis=1))
        first, second = [table_rows(tables, "span_inverse", 512 * block + 256 * i, 256) for i in range(2)]
        both = mul(jnp.concatenate([high, low], axis=0), first)
        fields.append(both[:ROWS] + both[ROWS:] + mul(high, second))
    (h0, h4), (r1, i1), (r2, i2), (r3, i3) = [(f[:, :128], f[:, 128:]) for f in fields]
    sums, differences = h0 + h4, h0 - h4
    evens = [sums + r2, differences - i2, sums - r2, differences + i2]
    odds = [r1 + r3, (r1 - r3 - i1 - i3) * HALF, i3 - i1, (r3 - r1 - i1 - i3) * HALF]
    for b in range(4):
        out_ref[0, 0, :, 128 * b : 128 * b + 128] = evens[b] + odds[b]
        out_ref[0, 0, :, 128 * b + 512 : 128 * b + 640] = evens[b] - odds[b]


def local(velocity):
    tables = jnp.asarray(np.concatenate(list(TABLES.values())))
    messages = pltpu.VMEM((CHUNKS, PEERS * TILE, 128), F32)
    return pl.pallas_call(
        kernel,
        out_shape=jax.ShapeDtypeStruct((1, 1, ROWS, NZ), F32),
        in_specs=[pl.BlockSpec(memory_space=pl.ANY)] * 2,
        out_specs=pl.BlockSpec(memory_space=pltpu.VMEM),
        scratch_shapes=[pltpu.VMEM(velocity.shape, F32), pltpu.VMEM(tables.shape, tables.dtype)]
        + [pltpu.VMEM((4, ROWS, 256), BF16)] * 2
        + [messages] * 4
        + [pltpu.SemaphoreType.DMA((n,)) for n in (3, 2 * CHUNKS, 2 * CHUNKS)],
        compiler_params=pltpu.CompilerParams(
            collective_id=0, has_side_effects=True, vmem_limit_bytes=107 * 512 * 1024
        ),
    )(velocity, tables)


def solution(mesh):
    return jax.shard_map(
        local, mesh=mesh, in_specs=(P("wall", "space", None),), out_specs=P("wall", None, "space", None), check_vma=False
    )
```
